128 devices in a mesh: date: 16 (over z, y_hi, core), tile: 8 (over y_lo, x).
Axes of the slice: x: 4, y: 4 (y_hi: 2, y_lo: 2; y = y_hi * 2 + y_lo), z: 4, core: 2. Of those that a mesh axis runs over, the one named last changes fastest.
Arguments:
- slc_re: float32 [64, 512, 1024], P('date', 'tile'), may hold values from -6 to 6
- slc_im: float32 [64, 512, 1024], P('date', 'tile'), may hold values from -6 to 6
- ref_dates: int32 [4], replicated, may hold values from 0 to 62, as said below
- pair_keep: int32 [4, 64], replicated, may hold values 0 or 1
- col_offsets: int32 [64], replicated, may hold values from 0 to 7
Outputs:
- coh_re: float32 [4, 64, 512, 1024], P(None, 'date', 'tile')
- coh_im: float32 [4, 64, 512, 1024], P(None, 'date', 'tile')
The draws below stay inside these ranges and needn't reach their ends.
Inputs may be any that keep to these rules, and one draw needn't show every extreme that they name: `ref_dates`: strictly increasing; the first is 0 and the last is 62.
All inputs are finite; a program needn't handle non-finite values.
Results may differ from the reference program's by a relative error of at most 0.0003.
Values sent between devices are 32-bit elements; how exact they have to be, the bound alone decides.
A program may use at most 128 MiB of HBM per device.

```python
import jax
import jax.numpy as jnp
from jax import lax

COLS = 1024
STEPS = 4
DATES = 64
ROWS = 512


def draw_ref_dates(key, part):
    key = jax.random.fold_in(key, 11)
    middle = jax.random.permutation(key, DATES - 3)[:STEPS - 2] + 1
    middle = jnp.sort(middle.astype(jnp.int32))
    first = jnp.zeros((1,), jnp.int32)
    last = jnp.full((1,), DATES - 2, jnp.int32)
    return jnp.concatenate([first, middle, last]).astype(jnp.int32)


def with_ends(result, rng, least, largest):
    shape = result.shape
    index_at = [jax.random.randint(jax.random.fold_in(rng, axis), (), 0, shape[axis]) for axis in range(len(shape))]
    result = result.at[tuple(index_at)].set(least)
    longest = shape.index(max(shape))
    index_at[longest] = (index_at[longest] + 1) % shape[longest]
    return result.at[tuple(index_at)].set(largest)


def block_levels(key, dims, pieces, least, largest):
    def one(position, parts):
        steps = jax.random.uniform(jax.random.fold_in(jax.random.fold_in(key, 6), position), (parts,), jnp.float32, least / len(pieces), largest / len(pieces))
        return jnp.repeat(jnp.exp(steps), dims[position] // parts).reshape((-1,) + (1,) * (len(dims) - position - 1))

    factor_of = one(*pieces[0])
    for cut in pieces[1:]:
        factor_of = factor_of * one(*cut)
    return factor_of


def scatter_about(rng, extent, width, bound, pieces=(), kind=jnp.bfloat16):
    values = width * jax.random.normal(rng, extent, jnp.float32)
    if pieces:
        values = values * block_levels(rng, extent, pieces, -0.22, 0.18)
    return jnp.clip(values, -bound, bound).astype(kind)


def setup_inputs(seed: int = 0) -> dict:
    streams_of = jax.random.split(jax.random.key(seed), 6)
    slc_re = scatter_about(streams_of[0], (DATES, ROWS, COLS), 1.0, 6.0, ((0, 16), (1, 8)), jnp.float32)
    slc_im = scatter_about(streams_of[1], (DATES, ROWS, COLS), 1.0, 6.0, ((0, 16), (1, 8)), jnp.float32)
    ref_dates = draw_ref_dates(jax.random.fold_in(streams_of[5], 71), 0)
    pair_keep = with_ends((jax.random.randint(streams_of[3], (STEPS, DATES), 0, 4) < 3).astype(jnp.int32), jax.random.fold_in(streams_of[3], 1), 0, 1)
    col_offsets = with_ends(jax.random.randint(streams_of[4], (DATES,), 0, 8), jax.random.fold_in(streams_of[4], 1), 0, 7).astype(jnp.int32)
    return dict(slc_re=slc_re, slc_im=slc_im, ref_dates=ref_dates, pair_keep=pair_keep, col_offsets=col_offsets)


def shift_columns(raw, offsets):
    cols = raw.shape[-1]
    padded = jnp.pad(raw, ((0, 0), (0, 0), (0, 0), (0, 8)))

    def one_date(plane, offset):
        return lax.dynamic_slice_in_dim(plane, offset.astype(jnp.int32), cols, 2)
    return jax.vmap(one_date, in_axes=(1, 0), out_axes=1)(padded, offsets)

def box_window(planes):
    rows = planes.shape[-2]
    cols = planes.shape[-1]
    padded = jnp.pad(planes, ((0, 0), (2, 2), (0, 0)))
    summed = padded[:, 0:rows]
    for k in range(1, 5):
        summed = summed + padded[:, k:k + rows]
    wide = jnp.pad(summed, ((0, 0), (0, 0), (10, 9)))
    total = wide[:, :, 0:cols]
    for k in range(1, 20):
        total = total + wide[:, :, k:k + cols]
    return total

def reference(slc_re, slc_im, ref_dates, pair_keep, col_offsets):
    raw = jnp.stack((slc_re, slc_im))
    secondary = shift_columns(raw, col_offsets)
    dates = jnp.arange(DATES, dtype=jnp.int32)
    out_re = []
    out_im = []
    for s in range(STEPS):
        ref = lax.dynamic_index_in_dim(raw, ref_dates[s].astype(jnp.int32), 1, keepdims=False)

        def per_date(j):
            sec = lax.dynamic_index_in_dim(secondary, j, 1, keepdims=False)
            ifg_re = ref[0] * sec[0] + ref[1] * sec[1]
            ifg_im = ref[1] * sec[0] - ref[0] * sec[1]
            pow_a = ref[0] * ref[0] + ref[1] * ref[1]
            pow_b = sec[0] * sec[0] + sec[1] * sec[1]
            boxed = box_window(jnp.stack((ifg_re, ifg_im, pow_a, pow_b)))
            scale = lax.rsqrt(boxed[2] * boxed[3] + 1e-06)
            return (boxed[0] * scale, boxed[1] * scale)
        part_re, part_im = lax.map(per_date, dates)
        valid = (pair_keep[s] == 1) & (dates > ref_dates[s])
        out_re.append(jnp.where(valid[:, None, None], part_re, jnp.float32(0.0)))
        out_im.append(jnp.where(valid[:, None, None], part_im, jnp.float32(0.0)))
    return (jnp.stack(out_re), jnp.stack(out_im))
```

```python
import jax
import jax.numpy as jnp
import numpy as np
from jax import lax
from jax.experimental import pallas as pl
from jax.experimental.pallas import tpu as pltpu
from jax.sharding import PartitionSpec as P

MESH = pl.DeviceIdType.MESH
DATE_DEV = 4
ROWS = 64
COLS = 1024
BLOCKS = COLS // 128
REFS = 3
VMEM_LIMIT = 56 * 2**20


def band_matrix():
    k = np.arange(128)[:, None]
    c = np.arange(128)[None, :]
    middle = (k >= c - 10) & (k <= c + 9)
    edge = ((c < 10) & (k >= 118 + c)) | ((c >= 119) & (k <= c - 119))
    half = np.concatenate([middle, edge], axis=1)
    return jnp.asarray(np.concatenate([half, half], axis=0), jnp.bfloat16)


def device(z, y, core):
    return {"date": (z * 2 + y) * 2 + core}


def spread_kernel(owners, dates_ref, re_ref, im_ref, refs, ref_edges, left, right, own_edges, twin, twin_edges, send, recv, edge_send, edge_recv):
    me = lax.axis_index("date")
    tile = lax.axis_index("tile")
    z, y, core = me // 4, (me // 2) % 2, me % 2
    tiles = lax.axis_size("tile")
    next_tile = {"tile": lax.rem(tile + 1, tiles)}
    last_tile = {"tile": lax.rem(tile + tiles - 1, tiles)}
    sibling = device(z, y, 1 - core)

    def owner(s):
        z0, y0 = owners[0]
        for k in range(1, REFS):
            z0 = jnp.where(s == k, owners[k][0], z0)
            y0 = jnp.where(s == k, owners[k][1], y0)
        return z0, y0

    barrier = pltpu.get_barrier_semaphore()

    def greet(target):
        pl.semaphore_signal(barrier, inc=1, device_id=target, device_id_type=MESH)

    greet(next_tile)
    greet(last_tile)
    greet(sibling)

    @pl.loop(1, 8)
    def _(k):
        greet({"date": lax.rem(me + 2 * k, 16)})

    for j in range(DATE_DEV):
        own_edges[j, 0:2] = re_ref[j, 0:2]
        own_edges[j, 2:4] = re_ref[j, ROWS - 2 : ROWS]
        own_edges[j, 4:6] = im_ref[j, 0:2]
        own_edges[j, 6:8] = im_ref[j, ROWS - 2 : ROWS]

    @pl.loop(0, REFS)
    def _(s):
        z0, y0 = owner(s)

        @pl.when((z == z0) & (y == y0))
        def _():
            slot = lax.rem(dates_ref[s], DATE_DEV)
            refs[s, 0] = re_ref[slot]
            refs[s, 1] = im_ref[slot]

    pl.semaphore_wait(barrier, 10)

    def edge_copy(k, source, target, to):
        return pltpu.make_async_remote_copy(
            src_ref=source, dst_ref=target, send_sem=edge_send.at[k], recv_sem=edge_recv.at[k], device_id=to, device_id_type=MESH
        )

    to_right = edge_copy(0, own_edges, left, next_tile)
    to_left = edge_copy(1, own_edges, right, last_tile)

    def copy(s, source, target, out, slot, to):
        return pltpu.make_async_remote_copy(
            src_ref=source, dst_ref=target, send_sem=send.at[s, out], recv_sem=recv.at[s, slot], device_id=to, device_id_type=MESH
        )

    def quarter(s, ring, plane):
        return refs.at[s, :, pl.ds(pl.multiple_of(plane * 32 + ring * 16, 16), 16), :]

    def whole(s):
        return copy(s, refs.at[s], twin.at[s], 7, 4, sibling)

    def edges_whole(s):
        return copy(s, ref_edges.at[s], twin_edges.at[s], 8, 6, sibling)

    def along(s, level):
        return copy(s, quarter(s, y, core), quarter(s, y, core), level, 0, device(level, y, core))

    def across(s, ring, slot):
        return copy(s, quarter(s, ring, core), quarter(s, ring, core), 4 if slot else 0, slot, device(z, 1 - y, core))

    def inward(s, ring, slot):
        return copy(s, quarter(s, ring, core), quarter(s, ring, core), 5 + slot, 2 + slot, sibling)

    def edges_out(s, k):
        return copy(s, ref_edges.at[s], ref_edges.at[s], 8 + k, 5, {"date": lax.rem(me + 2 * k, 16)})

    def roles(s):
        z0, y0 = owner(s)
        source = (z == z0) & (y == y0)
        relay = (z == z0) & (y != y0)
        beyond = z > z0
        return z0, y0, source, relay, beyond

    def to_levels(s, act):
        z0, _ = owner(s)

        @pl.loop(1, 4)
        def _(level):
            @pl.when(level > z0)
            def _():
                act(along(s, level))

    def to_all(s, act):
        z0, _ = owner(s)

        @pl.loop(1, 8)
        def _(k):
            @pl.when(lax.rem(me + 2 * k, 16) // 4 >= z0)
            def _():
                act(edges_out(s, k))

    @pl.loop(0, REFS)
    def _(s):
        @pl.when(roles(s)[2])
        def _():
            whole(s).start()

    to_right.start()
    to_left.start()

    @pl.loop(0, REFS)
    def _(s):
        z0, y0, source, relay, beyond = roles(s)

        @pl.when(source)
        def _():
            whole(s).wait()
            mine = lax.rem(dates_ref[s] // DATE_DEV, 2) == core
            refs[s] = jnp.where(mine, refs[s], twin[s])
            across(s, 1 - y, 0).start()
            to_levels(s, lambda c: c.start())
            across(s, y, 1).start()

    to_right.wait_recv()
    to_left.wait_recv()

    @pl.loop(0, REFS)
    def _(s):
        @pl.when(roles(s)[2])
        def _():
            slot = lax.rem(dates_ref[s], DATE_DEV)
            ref_edges[s, 0:2] = left[slot, 2:4]
            ref_edges[s, 2:4] = right[slot, 0:2]
            ref_edges[s, 4:6] = left[slot, 6:8]
            ref_edges[s, 6:8] = right[slot, 4:6]
            edges_whole(s).start()

    @pl.loop(0, REFS)
    def _(s):
        @pl.when(roles(s)[2])
        def _():
            edges_whole(s).wait()
            mine = lax.rem(dates_ref[s] // DATE_DEV, 2) == core
            ref_edges[s] = jnp.where(mine, ref_edges[s], twin_edges[s])
            to_all(s, lambda c: c.start())

    @pl.loop(0, REFS)
    def _(s):
        z0, y0, source, relay, beyond = roles(s)

        @pl.when(relay | beyond)
        def _():
            copy(s, quarter(s, y, core), quarter(s, y, core), 0, 0, sibling).wait_recv()

            @pl.when(relay)
            def _():
                to_levels(s, lambda c: c.start())

            @pl.when(beyond)
            def _():
                across(s, y, 1).start()

            inward(s, y, 0).start()

    @pl.loop(0, REFS)
    def _(s):
        z0, y0, source, relay, beyond = roles(s)

        @pl.when(relay | beyond)
        def _():
            copy(s, quarter(s, 1 - y, core), quarter(s, 1 - y, core), 0, 1, sibling).wait_recv()
            inward(s, 1 - y, 1).start()

    @pl.loop(0, REFS)
    def _(s):
        z0, y0, source, relay, beyond = roles(s)

        @pl.when(relay | beyond)
        def _():
            edges_out(s, 1).wait_recv()
            copy(s, quarter(s, y, 1 - core), quarter(s, y, 1 - core), 0, 2, sibling).wait_recv()
            copy(s, quarter(s, 1 - y, 1 - core), quarter(s, 1 - y, 1 - core), 0, 3, sibling).wait_recv()
            inward(s, y, 0).wait_send()
            inward(s, 1 - y, 1).wait_send()

        @pl.when(source | relay)
        def _():
            to_levels(s, lambda c: c.wait_send())

        @pl.when(source)
        def _():
            across(s, 1 - y, 0).wait_send()
            to_all(s, lambda c: c.wait_send())

        @pl.when(source | beyond)
        def _():
            across(s, y, 1).wait_send()

    to_right.wait_send()
    to_left.wait_send()


def spread(first, second, number):
    owners = [(chip // 2, chip % 2) for chip in (0, first, second)]

    def kernel(*refs):
        spread_kernel(owners, *refs)

    vmem = pl.BlockSpec(memory_space=pltpu.VMEM)

    def call(dates, slc_re, slc_im):
        return pl.pallas_call(
            kernel,
            out_shape=(
                jax.ShapeDtypeStruct((REFS, 2, ROWS, COLS), jnp.float32),
                jax.ShapeDtypeStruct((REFS, 8, COLS), jnp.float32),
                jax.ShapeDtypeStruct((DATE_DEV, 8, COLS), jnp.float32),
                jax.ShapeDtypeStruct((DATE_DEV, 8, COLS), jnp.float32),
            ),
            in_specs=[pl.BlockSpec(memory_space=pltpu.SMEM), vmem, vmem],
            out_specs=(vmem, vmem, vmem, vmem),
            scratch_shapes=[
                pltpu.VMEM((DATE_DEV, 8, COLS), jnp.float32),
                pltpu.VMEM((REFS, 2, ROWS, COLS), jnp.float32),
                pltpu.VMEM((REFS, 8, COLS), jnp.float32),
                pltpu.SemaphoreType.DMA((REFS, 16)),
                pltpu.SemaphoreType.DMA((REFS, 7)),
                pltpu.SemaphoreType.DMA((2,)),
                pltpu.SemaphoreType.DMA((2,)),
            ],
            compiler_params=pltpu.CompilerParams(collective_id=number, has_side_effects=True, vmem_limit_bytes=VMEM_LIMIT),
            name=f"spread_{first}_{second}",
        )(dates, slc_re, slc_im)

    return call


def pick_kernel(dates_ref, pick_ref):
    first = dates_ref[1] // (2 * DATE_DEV)
    second = dates_ref[2] // (2 * DATE_DEV)
    pick_ref[0] = (first * (17 - first)) // 2 + (second - first)


def compute_kernel(
    dates_ref, keep_ref, offsets_ref, re_ref, im_ref, left, right, refs, ref_edges, band, out_re, out_im, a_ext, b_ext, prod, wide, pow_a, pow_b
):
    j = pl.program_id(0)
    s = pl.program_id(1)
    me = lax.axis_index("date")
    tile = lax.axis_index("tile")
    date = me * DATE_DEV + j
    has_top = (tile > 0).astype(jnp.float32)
    has_bottom = (tile < lax.axis_size("tile") - 1).astype(jnp.float32)
    valid = (keep_ref[s, date] == 1) & (date > dates_ref[s])

    def lay(ext, plane, rows, top, bottom):
        top = top * has_top
        bottom = bottom * has_bottom
        for g in range(BLOCKS):
            cut = slice(128 * g, 128 * g + 128)
            ext[plane, g, 0:2] = top[:, cut]
            ext[plane, g, 2 : ROWS + 2] = rows[:, cut]
            ext[plane, g, ROWS + 2 : ROWS + 4] = bottom[:, cut]

    def widen(count):
        for g in range(BLOCKS):
            for p in range(count):
                total = prod[p, g, 0:ROWS]
                for k in range(1, 5):
                    total = total + prod[p, g, k : k + ROWS]
                high = total.astype(jnp.bfloat16)
                low = (total - high.astype(jnp.float32)).astype(jnp.bfloat16)
                wide[g, p * ROWS : (p + 1) * ROWS, 0:128] = high
                wide[g, p * ROWS : (p + 1) * ROWS, 128:256] = low

    def columns(count):
        rows = count * ROWS
        lhs = wide[:, 0:rows, :].reshape(BLOCKS * rows, 256)
        return jnp.dot(lhs, band[...], preferred_element_type=jnp.float32).reshape(BLOCKS, rows, 256)

    lane = lax.broadcasted_iota(jnp.int32, (ROWS, 128), 1)

    def joined(sums, g, p):
        rows = slice(p * ROWS, (p + 1) * ROWS)
        zero = jnp.zeros((ROWS, 128), jnp.float32)
        before = sums[g - 1, rows, 128:256] if g > 0 else zero
        after = sums[g + 1, rows, 128:256] if g < BLOCKS - 1 else zero
        return sums[g, rows, 0:128] + jnp.where(lane < 64, before, after)

    def power(ext, out):
        for g in range(BLOCKS):
            prod[0, g, 0:72] = ext[0, g] * ext[0, g] + ext[1, g] * ext[1, g]
        widen(1)
        sums = columns(1)
        for g in range(BLOCKS):
            out[g] = joined(sums, g, 0)

    @pl.when((j == 0) & (s < REFS))
    def _():
        at = jnp.minimum(s, REFS - 1)
        edges = ref_edges[at]
        lay(a_ext.at[s], 0, refs[at, 0], edges[0:2], edges[2:4])
        lay(a_ext.at[s], 1, refs[at, 1], edges[4:6], edges[6:8])
        power(a_ext.at[s], pow_a.at[s])

    @pl.when((s == REFS) & valid)
    def _():
        edges_left = left[DATE_DEV - 2]
        edges_right = right[DATE_DEV - 2]
        lay(a_ext.at[s], 0, re_ref[DATE_DEV - 2], edges_left[2:4], edges_right[0:2])
        lay(a_ext.at[s], 1, im_ref[DATE_DEV - 2], edges_left[6:8], edges_right[4:6])
        power(a_ext.at[s], pow_a.at[s])

    @pl.when(s == 0)
    def _():
        offset = offsets_ref[date]
        turn = lax.rem(COLS - offset, COLS)

        def shifted(x):
            column = lax.broadcasted_iota(jnp.int32, x.shape, 1)
            return jnp.where(column < COLS - offset, pltpu.roll(x, turn, 1), 0.0)

        edges_left = shifted(left[j])
        edges_right = shifted(right[j])
        lay(b_ext, 0, shifted(re_ref[j]), edges_left[2:4], edges_right[0:2])
        lay(b_ext, 1, shifted(im_ref[j]), edges_left[6:8], edges_right[4:6])
        power(b_ext, pow_b)

    @pl.when(valid)
    def _():
        for g in range(BLOCKS):
            a_re, a_im = a_ext[s, 0, g], a_ext[s, 1, g]
            b_re, b_im = b_ext[0, g], b_ext[1, g]
            prod[0, g] = a_re * b_re + a_im * b_im
            prod[1, g] = a_im * b_re - a_re * b_im
        widen(2)
        sums = columns(2)
        for g in range(BLOCKS):
            scale = lax.rsqrt(pow_a[s, g] * pow_b[g] + 1e-06)
            out_re[0, 0, :, 128 * g : 128 * g + 128] = joined(sums, g, 0) * scale
            out_im[0, 0, :, 128 * g : 128 * g + 128] = joined(sums, g, 1) * scale

    @pl.when(jnp.logical_not(valid))
    def _():
        out_re[...] = jnp.zeros_like(out_re)
        out_im[...] = jnp.zeros_like(out_im)


def compute(dates, keep, offsets, slc_re, slc_im, left, right, refs, ref_edges):
    steps = REFS + 1
    smem = pl.BlockSpec(memory_space=pltpu.SMEM)
    vmem = pl.BlockSpec(memory_space=pltpu.VMEM)
    shape = jax.ShapeDtypeStruct((steps, DATE_DEV, ROWS, COLS), jnp.float32)
    out = pl.BlockSpec((1, 1, ROWS, COLS), lambda j, s: (s, j, 0, 0))
    return pl.pallas_call(
        compute_kernel,
        grid=(DATE_DEV, steps),
        out_shape=(shape, shape),
        in_specs=[smem, smem, smem] + [vmem] * 7,
        out_specs=(out, out),
        scratch_shapes=[
            pltpu.VMEM((steps, 2, BLOCKS, 72, 128), jnp.float32),
            pltpu.VMEM((2, BLOCKS, 72, 128), jnp.float32),
            pltpu.VMEM((2, BLOCKS, 72, 128), jnp.float32),
            pltpu.VMEM((BLOCKS, 2 * ROWS, 256), jnp.bfloat16),
            pltpu.VMEM((steps, BLOCKS, ROWS, 128), jnp.float32),
            pltpu.VMEM((BLOCKS, ROWS, 128), jnp.float32),
        ],
        compiler_params=pltpu.CompilerParams(vmem_limit_bytes=VMEM_LIMIT),
        name="coherence",
    )(dates, keep, offsets, slc_re, slc_im, left, right, refs, ref_edges, band_matrix())


def body(slc_re, slc_im, ref_dates, pair_keep, col_offsets):
    pick = pl.pallas_call(
        pick_kernel,
        out_shape=jax.ShapeDtypeStruct((1,), jnp.int32),
        in_specs=[pl.BlockSpec(memory_space=pltpu.SMEM)],
        out_specs=pl.BlockSpec(memory_space=pltpu.SMEM),
        name="pick",
    )(ref_dates)[0]
    pairs = [(first, second) for first in range(8) for second in range(first, 8)]
    branches = [spread(first, second, number) for number, (first, second) in enumerate(pairs)]
    refs, ref_edges, left, right = lax.switch(pick, branches, ref_dates, slc_re, slc_im)
    return compute(ref_dates, pair_keep, col_offsets, slc_re, slc_im, left, right, refs, ref_edges)


def solution(mesh):
    placed = (P("date", "tile", None), P("date", "tile", None), P(), P(), P())
    return jax.shard_map(
        body,
        mesh=mesh,
        in_specs=placed,
        out_specs=(P(None, "date", "tile", None), P(None, "date", "tile", None)),
        check_vma=False,
    )
```

```python
import jax
import jax.numpy as jnp
import numpy as np
from jax import lax
from jax.experimental import pallas as pl
from jax.experimental.pallas import tpu as pltpu
from jax.sharding import PartitionSpec as P

MESH = pl.DeviceIdType.MESH
DATE_DEV = 4
ROWS = 64
COLS = 1024
BLOCKS = COLS // 128
REFS = 3
STEPS = 4
VMEM_LIMIT = 56 * 2**20


def band_matrix():
    k = np.arange(128)[:, None]
    c = np.arange(128)[None, :]
    middle = (k >= c - 10) & (k <= c + 9)
    edge = ((c < 10) & (k >= 118 + c)) | ((c >= 119) & (k <= c - 119))
    half = np.concatenate([middle, edge], axis=1)
    return jnp.asarray(np.concatenate([half, half], axis=0), jnp.bfloat16)


CHIPS = 8


def spread_kernel(
    dates_ref,
    re_ref,
    im_ref,
    refs,
    ref_edges,
    left,
    right,
    own_edges,
    packed,
    outward,
    halves,
    first_half,
    merged,
    pieces,
    pair_send,
    pair_recv,
    edge_send,
    edge_recv,
    first_send,
    first_recv,
    gather_send,
    gather_recv,
    spread_send,
    spread_recv,
    inward_send,
    inward_recv,
    rim_send,
    rim_recv,
    rim_in_send,
    rim_in_recv,
):
    me = lax.axis_index("date")
    tile = lax.axis_index("tile")
    chip, core = me // 2, me % 2
    tiles = lax.axis_size("tile")
    next_tile = {"tile": lax.rem(tile + 1, tiles)}
    last_tile = {"tile": lax.rem(tile + tiles - 1, tiles)}
    sibling = {"date": chip * 2 + 1 - core}

    def same_core(k):
        return {"date": k * 2 + core}

    def other(i):
        return lax.rem(chip + i, CHIPS)

    def remote(source, target, send, recv, to):
        return pltpu.make_async_remote_copy(src_ref=source, dst_ref=target, send_sem=send, recv_sem=recv, device_id=to, device_id_type=MESH)

    barrier = pltpu.get_barrier_semaphore()

    def greet(target):
        pl.semaphore_signal(barrier, inc=1, device_id=target, device_id_type=MESH)

    @pl.loop(1, CHIPS)
    def _(i):
        greet(same_core(other(i)))

    greet(next_tile)
    greet(last_tile)
    greet(sibling)

    def half(slot, c):
        rows = pl.ds(pl.multiple_of(c * 32, 32), 32)
        return re_ref[slot, rows].reshape(4, 8, COLS), im_ref[slot, rows].reshape(4, 8, COLS)

    for s in range(1, REFS):
        slot = lax.rem(dates_ref[s], DATE_DEV)
        halves[core, s - 1, 0:4], halves[core, s - 1, 4:8] = half(slot, core)
        outward[s - 1, 0:4], outward[s - 1, 4:8] = half(slot, 1 - core)

    @pl.when(me == 0)
    def _():
        first_half[0:4], first_half[4:8] = half(0, 0)
        outward[REFS - 1, 0:4], outward[REFS - 1, 4:8] = half(0, 1)

    for j in range(DATE_DEV):
        own_edges[j, 0:2] = re_ref[j, 0:2]
        own_edges[j, 2:4] = re_ref[j, ROWS - 2 : ROWS]
        own_edges[j, 4:6] = im_ref[j, 0:2]
        own_edges[j, 6:8] = im_ref[j, ROWS - 2 : ROWS]

    pl.semaphore_wait(barrier, 10)

    to_sibling = remote(outward.at[pl.ds(0, 2)], halves.at[core], pair_send.at[0], pair_recv.at[0], sibling)
    first_to_sibling = remote(outward.at[REFS - 1], first_half, pair_send.at[1], pair_recv.at[1], sibling)
    to_sibling.start()

    def first_out(k):
        return remote(first_half.at[k], refs.at[0, core, k], first_send.at[k], first_recv.at[0], same_core(k))

    def first_all():
        refs[0, core, 0] = first_half[0]

        @pl.loop(1, CHIPS)
        def _(k):
            first_out(k).start()

    @pl.when(me == 0)
    def _():
        first_to_sibling.start()
        first_all()

    to_right = remote(own_edges, left, edge_send.at[0], edge_recv.at[0], next_tile)
    to_left = remote(own_edges, right, edge_send.at[1], edge_recv.at[1], last_tile)
    to_right.start()
    to_left.start()

    to_sibling.wait_recv()
    for s in range(1, REFS):
        owner_core = lax.rem(dates_ref[s] // DATE_DEV, 2)
        merged[:, s - 1] = halves[owner_core, s - 1]

    def gather(k):
        return remote(merged.at[k], pieces.at[chip], gather_send.at[k], gather_recv.at[chip], same_core(k))

    def gathered(k):
        return remote(merged.at[k], pieces.at[k], gather_send.at[k], gather_recv.at[k], same_core(k))

    @pl.loop(1, CHIPS)
    def _(i):
        gather(other(i)).start()

    @pl.when(me == 1)
    def _():
        first_to_sibling.wait_recv()
        first_all()

    def part(n, k):
        return refs.at[0, core, k] if n == 0 else refs.at[pl.ds(1, 2), core, k]

    def spread_out(n, k):
        return remote(part(n, chip), part(n, chip), spread_send.at[n, k], spread_recv.at[n, chip], same_core(k))

    def spread_in(n, k):
        return remote(part(n, k), part(n, k), spread_send.at[n, k], spread_recv.at[n, k], same_core(k))

    def inward(n, k):
        return remote(part(n, k), part(n, k), inward_send.at[n, k], inward_recv.at[n, k], sibling)

    def inward_in(n, k):
        there = refs.at[0, 1 - core, k] if n == 0 else refs.at[pl.ds(1, 2), 1 - core, k]
        return remote(there, there, inward_send.at[n, k], inward_recv.at[n, k], sibling)

    def spread_all(n):
        @pl.loop(1, CHIPS)
        def _(i):
            spread_out(n, other(i)).start()

        inward(n, chip).start()

    @pl.when(chip > 0)
    def _():
        first_out(chip).wait_recv()

    spread_all(0)
    pieces[chip] = merged[chip]

    @pl.loop(1, CHIPS)
    def _(i):
        gathered(other(i)).wait_recv()

    for s in range(1, REFS):
        refs[s, core, chip] = pieces[dates_ref[s] // (2 * DATE_DEV), s - 1]
    spread_all(1)

    below = (core == 0) & (lax.rem(chip, 4) == 0)
    above = (core == 1) & (lax.rem(chip, 4) == 3)
    own_kind = jnp.where(core == 0, 0, 2) + chip // 4

    def rim_over(to):
        return remote(packed, ref_edges.at[own_kind], rim_send.at[0], rim_recv.at[4], to)

    @pl.when(below)
    def _():
        for s in range(REFS):
            packed[2 * s : 2 * s + 2] = refs[s, core, chip, 0:2]
        packed[6:8] = jnp.zeros((2, COLS), jnp.float32)
        rim_over(last_tile).start()

    @pl.when(above)
    def _():
        for s in range(REFS):
            packed[2 * s : 2 * s + 2] = refs[s, core, chip, 6:8]
        packed[6:8] = jnp.zeros((2, COLS), jnp.float32)
        rim_over(next_tile).start()

    def rim_out(k):
        return remote(ref_edges.at[own_kind], ref_edges.at[own_kind], rim_send.at[1 + k], rim_recv.at[own_kind], same_core(k))

    def rim_in(kind):
        return remote(ref_edges.at[kind], ref_edges.at[kind], rim_send.at[0], rim_recv.at[kind], sibling)

    def rim_inward(kind):
        return remote(ref_edges.at[kind], ref_edges.at[kind], rim_in_send.at[kind], rim_in_recv.at[kind], sibling)

    @pl.when(below | above)
    def _():
        rim_over(next_tile).wait_recv()

        @pl.loop(1, CHIPS)
        def _(i):
            rim_out(other(i)).start()

        rim_inward(own_kind).start()

    for n in range(2):

        @pl.loop(1, CHIPS)
        def _(i):
            k = other(i)
            spread_in(n, k).wait_recv()
            inward(n, k).start()

    @pl.loop(0, 2)
    def _(m):
        kind = core * 2 + m

        @pl.when(jnp.logical_not((below | above) & (kind == own_kind)))
        def _():
            rim_in(kind).wait_recv()
            rim_inward(kind).start()

    for n in range(2):

        @pl.loop(0, CHIPS)
        def _(k):
            inward_in(n, k).wait_recv()

    @pl.loop(0, 2)
    def _(m):
        rim_inward((1 - core) * 2 + m).wait_recv()
        rim_inward(core * 2 + m).wait_send()

    to_right.wait()
    to_left.wait()
    to_sibling.wait_send()

    @pl.when(me == 0)
    def _():
        first_to_sibling.wait_send()

    @pl.when(chip == 0)
    def _():
        @pl.loop(1, CHIPS)
        def _(k):
            first_out(k).wait_send()

    @pl.when(below | above)
    def _():
        rim_over(next_tile).wait_send()

        @pl.loop(1, CHIPS)
        def _(i):
            rim_out(other(i)).wait_send()

    @pl.loop(1, CHIPS)
    def _(i):
        gather(other(i)).wait_send()

    for n in range(2):

        @pl.loop(1, CHIPS)
        def _(i):
            spread_out(n, other(i)).wait_send()
            inward(n, other(i)).wait_send()

        inward(n, chip).wait_send()


def spread(dates, slc_re, slc_im):
    vmem = pl.BlockSpec(memory_space=pltpu.VMEM)
    f32 = jnp.float32
    dma = pltpu.SemaphoreType.DMA
    return pl.pallas_call(
        spread_kernel,
        out_shape=(
            jax.ShapeDtypeStruct((REFS, 2, CHIPS, 8, COLS), f32),
            jax.ShapeDtypeStruct((4, 8, COLS), f32),
            jax.ShapeDtypeStruct((DATE_DEV, 8, COLS), f32),
            jax.ShapeDtypeStruct((DATE_DEV, 8, COLS), f32),
        ),
        in_specs=[pl.BlockSpec(memory_space=pltpu.SMEM), vmem, vmem],
        out_specs=(vmem, vmem, vmem, vmem),
        scratch_shapes=[
            pltpu.VMEM((DATE_DEV, 8, COLS), f32),
            pltpu.VMEM((8, COLS), f32),
            pltpu.VMEM((REFS, CHIPS, 8, COLS), f32),
            pltpu.VMEM((2, 2, CHIPS, 8, COLS), f32),
            pltpu.VMEM((CHIPS, 8, COLS), f32),
            pltpu.VMEM((CHIPS, 2, 8, COLS), f32),
            pltpu.VMEM((CHIPS, 2, 8, COLS), f32),
            dma((2,)),
            dma((2,)),
            dma((2,)),
            dma((2,)),
            dma((CHIPS,)),
            dma((1,)),
            dma((CHIPS,)),
            dma((CHIPS,)),
            dma((2, CHIPS)),
            dma((2, CHIPS)),
            dma((2, CHIPS)),
            dma((2, CHIPS)),
            dma((CHIPS + 1,)),
            dma((5,)),
            dma((4,)),
            dma((4,)),
        ],
        compiler_params=pltpu.CompilerParams(collective_id=0, has_side_effects=True, vmem_limit_bytes=VMEM_LIMIT),
        name="spread",
    )(dates, slc_re, slc_im)


def compute_kernel(
    dates_ref,
    keep_ref,
    offsets_ref,
    re_hbm,
    im_hbm,
    left_hbm,
    right_hbm,
    refs_hbm,
    ref_edges_hbm,
    band,
    out_re,
    out_im,
    re_ref,
    im_ref,
    left,
    right,
    refs,
    ref_edges,
    zeros,
    stage,
    a_ext,
    b_ext,
    prod,
    wide,
    pow_a,
    pow_b,
    date_sems,
    edge_sems,
    ref_sems,
    out_sems,
):
    me = lax.axis_index("date")
    tile = lax.axis_index("tile")
    has_top = (tile > 0).astype(jnp.float32)
    has_bottom = (tile < lax.axis_size("tile") - 1).astype(jnp.float32)
    outs = (out_re, out_im)

    def edge_loads():
        sources = ((left_hbm, left), (right_hbm, right), (ref_edges_hbm, ref_edges))
        return [pltpu.make_async_copy(a, b, edge_sems.at[k]) for k, (a, b) in enumerate(sources)]

    def date_loads(j):
        sources = ((re_hbm, re_ref), (im_hbm, im_ref))
        return [pltpu.make_async_copy(a.at[j], b.at[j], date_sems.at[k, j]) for k, (a, b) in enumerate(sources)]

    def ref_load(s):
        return pltpu.make_async_copy(refs_hbm.at[s], refs.at[s], ref_sems.at[s])

    def zero_out(s, j, p):
        return pltpu.make_async_copy(zeros, outs[p].at[s, j], out_sems.at[p, s, j])

    def value_out(s, j, p):
        return pltpu.make_async_copy(stage.at[p, s, j], outs[p].at[s, j], out_sems.at[p, s, j])

    def valid(s, j):
        date = me * DATE_DEV + j
        return (keep_ref[s, date] == 1) & (date > dates_ref[s])

    for c in edge_loads():
        c.start()

    @pl.loop(0, DATE_DEV)
    def _(j):
        for c in date_loads(j):
            c.start()

    @pl.loop(0, REFS)
    def _(s):
        ref_load(s).start()

    zeros[...] = jnp.zeros_like(zeros)

    @pl.loop(0, STEPS)
    def _(s):
        @pl.loop(0, DATE_DEV)
        def _(j):
            @pl.when(jnp.logical_not(valid(s, j)))
            def _():
                zero_out(s, j, 0).start()
                zero_out(s, j, 1).start()

    def lay(ext, plane, rows, top, bottom):
        top = top * has_top
        bottom = bottom * has_bottom
        for g in range(BLOCKS):
            cut = slice(128 * g, 128 * g + 128)
            ext[plane, g, 0:2] = top[:, cut]
            ext[plane, g, 2 : ROWS + 2] = rows[:, cut]
            ext[plane, g, ROWS + 2 : ROWS + 4] = bottom[:, cut]

    def edge_rows(tile_rows, at):
        return jnp.where(at == 0, tile_rows[0:2], jnp.where(at == 1, tile_rows[2:4], tile_rows[4:6]))

    def widen(count):
        for g in range(BLOCKS):
            for p in range(count):
                total = prod[p, g, 0:ROWS]
                for k in range(1, 5):
                    total = total + prod[p, g, k : k + ROWS]
                high = total.astype(jnp.bfloat16)
                low = (total - high.astype(jnp.float32)).astype(jnp.bfloat16)
                wide[g, p * ROWS : (p + 1) * ROWS, 0:128] = high
                wide[g, p * ROWS : (p + 1) * ROWS, 128:256] = low

    def columns(count):
        rows = count * ROWS
        lhs = wide[:, 0:rows, :].reshape(BLOCKS * rows, 256)
        return jnp.dot(lhs, band[...], preferred_element_type=jnp.float32).reshape(BLOCKS, rows, 256)

    lane = lax.broadcasted_iota(jnp.int32, (ROWS, 128), 1)

    def joined(sums, g, p):
        rows = slice(p * ROWS, (p + 1) * ROWS)
        zero = jnp.zeros((ROWS, 128), jnp.float32)
        before = sums[g - 1, rows, 128:256] if g > 0 else zero
        after = sums[g + 1, rows, 128:256] if g < BLOCKS - 1 else zero
        return sums[g, rows, 0:128] + jnp.where(lane < 64, before, after)

    def power(ext, out):
        for g in range(BLOCKS):
            prod[0, g] = ext[0, g] * ext[0, g] + ext[1, g] * ext[1, g]
        widen(1)
        sums = columns(1)
        for g in range(BLOCKS):
            out[g] = joined(sums, g, 0)

    def pair(s, j):
        for g in range(BLOCKS):
            a_re, a_im = a_ext[0, g], a_ext[1, g]
            b_re, b_im = b_ext[j, 0, g], b_ext[j, 1, g]
            prod[0, g] = a_re * b_re + a_im * b_im
            prod[1, g] = a_im * b_re - a_re * b_im
        widen(2)
        sums = columns(2)
        for g in range(BLOCKS):
            scale = lax.rsqrt(pow_a[g] * pow_b[j, g] + 1e-06)
            for p in range(2):
                stage[p, s, j, :, 128 * g : 128 * g + 128] = joined(sums, g, p) * scale
        value_out(s, j, 0).start()
        value_out(s, j, 1).start()

    for c in edge_loads():
        c.wait()

    @pl.loop(0, DATE_DEV)
    def _(j):
        for c in date_loads(j):
            c.wait()
        offset = offsets_ref[me * DATE_DEV + j]
        turn = lax.rem(COLS - offset, COLS)

        def shifted(x):
            column = lax.broadcasted_iota(jnp.int32, x.shape, 1)
            return jnp.where(column < COLS - offset, pltpu.roll(x, turn, 1), 0.0)

        edges_left = shifted(left[j])
        edges_right = shifted(right[j])
        lay(b_ext.at[j], 0, shifted(re_ref[j]), edges_left[2:4], edges_right[0:2])
        lay(b_ext.at[j], 1, shifted(im_ref[j]), edges_left[6:8], edges_right[4:6])
        power(b_ext.at[j], pow_b.at[j])

    @pl.loop(0, STEPS)
    def _(s):
        @pl.when(s < REFS)
        def _():
            at = jnp.minimum(s, REFS - 1)
            ref_load(at).wait()
            for p in range(2):
                rows = refs[at, :, 4 * p : 4 * p + 4].reshape(ROWS, COLS)
                lay(a_ext, p, rows, edge_rows(ref_edges[2 + p], at), edge_rows(ref_edges[p], at))

        @pl.when(s == REFS)
        def _():
            edges_left = left[DATE_DEV - 2]
            edges_right = right[DATE_DEV - 2]
            lay(a_ext, 0, re_ref[DATE_DEV - 2], edges_left[2:4], edges_right[0:2])
            lay(a_ext, 1, im_ref[DATE_DEV - 2], edges_left[6:8], edges_right[4:6])

        some = valid(s, 0) | valid(s, 1) | valid(s, 2) | valid(s, 3)

        @pl.when(some)
        def _():
            power(a_ext, pow_a)

        @pl.loop(0, DATE_DEV)
        def _(j):
            @pl.when(valid(s, j))
            def _():
                pair(s, j)

    @pl.loop(0, STEPS)
    def _(s):
        @pl.loop(0, DATE_DEV)
        def _(j):
            value_out(s, j, 0).wait()
            value_out(s, j, 1).wait()


def compute(dates, keep, offsets, slc_re, slc_im, left, right, refs, ref_edges):
    smem = pl.BlockSpec(memory_space=pltpu.SMEM)
    vmem = pl.BlockSpec(memory_space=pltpu.VMEM)
    hbm = pl.BlockSpec(memory_space=pl.ANY)
    shape = jax.ShapeDtypeStruct((STEPS, DATE_DEV, ROWS, COLS), jnp.float32)
    f32 = jnp.float32
    return pl.pallas_call(
        compute_kernel,
        out_shape=(shape, shape),
        in_specs=[smem] * 3 + [hbm] * 6 + [vmem],
        out_specs=(hbm, hbm),
        scratch_shapes=[
            pltpu.VMEM((DATE_DEV, ROWS, COLS), f32),
            pltpu.VMEM((DATE_DEV, ROWS, COLS), f32),
            pltpu.VMEM((DATE_DEV, 8, COLS), f32),
            pltpu.VMEM((DATE_DEV, 8, COLS), f32),
            pltpu.VMEM((REFS, 2, CHIPS, 8, COLS), f32),
            pltpu.VMEM((4, 8, COLS), f32),
            pltpu.VMEM((ROWS, COLS), f32),
            pltpu.VMEM((2, STEPS, DATE_DEV, ROWS, COLS), f32),
            pltpu.VMEM((2, BLOCKS, 72, 128), f32),
            pltpu.VMEM((DATE_DEV, 2, BLOCKS, 72, 128), f32),
            pltpu.VMEM((2, BLOCKS, 72, 128), f32),
            pltpu.VMEM((BLOCKS, 2 * ROWS, 256), jnp.bfloat16),
            pltpu.VMEM((BLOCKS, ROWS, 128), f32),
            pltpu.VMEM((DATE_DEV, BLOCKS, ROWS, 128), f32),
            pltpu.SemaphoreType.DMA((2, DATE_DEV)),
            pltpu.SemaphoreType.DMA((3,)),
            pltpu.SemaphoreType.DMA((REFS,)),
            pltpu.SemaphoreType.DMA((2, STEPS, DATE_DEV)),
        ],
        compiler_params=pltpu.CompilerParams(vmem_limit_bytes=VMEM_LIMIT),
        name="coherence",
    )(dates, keep, offsets, slc_re, slc_im, left, right, refs, ref_edges, band_matrix())


def body(slc_re, slc_im, ref_dates, pair_keep, col_offsets):
    refs, ref_edges, left, right = spread(ref_dates, slc_re, slc_im)
    return compute(ref_dates, pair_keep, col_offsets, slc_re, slc_im, left, right, refs, ref_edges)


def solution(mesh):
    placed = (P("date", "tile", None), P("date", "tile", None), P(), P(), P())
    return jax.shard_map(
        body,
        mesh=mesh,
        in_specs=placed,
        out_specs=(P(None, "date", "tile", None), P(None, "date", "tile", None)),
        check_vma=False,
    )
```

```python
import jax
import jax.numpy as jnp
from jax import lax
from jax.experimental import pallas as pl
from jax.experimental.pallas import tpu as pltpu
from jax.sharding import PartitionSpec as P

MESH = pl.DeviceIdType.MESH
DATE_DEV = 4
ROWS = 64
COLS = 1024
BLOCKS = COLS // 128
REFS = 3
STEPS = 4
VMEM_LIMIT = 24 * 2**20


def band_matrix():
    k = lax.rem(lax.broadcasted_iota(jnp.int32, (256, 256), 0), 128)
    c = lax.broadcasted_iota(jnp.int32, (256, 256), 1)
    within = (c < 128) & (k >= c - 10) & (k <= c + 9)
    after = (c >= 128) & (c < 138) & (k >= c - 10)
    before = (c >= 247) & (k <= c - 247)
    return jnp.where(within | after | before, 1.0, 0.0).astype(jnp.bfloat16)


def lay(ext, plane, rows, top, bottom):
    for g in range(BLOCKS):
        cut = slice(128 * g, 128 * g + 128)
        ext[plane, g, 0:2] = top[:, cut]
        ext[plane, g, 2 : ROWS + 2] = rows[:, cut]
        ext[plane, g, ROWS + 2 : ROWS + 4] = bottom[:, cut]


def widen(prod, wide, count):
    for g in range(BLOCKS):
        for p in range(count):
            total = prod[p, g, 0:ROWS]
            for k in range(1, 5):
                total = total + prod[p, g, k : k + ROWS]
            high = total.astype(jnp.bfloat16)
            low = (total - high.astype(jnp.float32)).astype(jnp.bfloat16)
            wide[g, p * ROWS : (p + 1) * ROWS, 0:128] = high
            wide[g, p * ROWS : (p + 1) * ROWS, 128:256] = low


def columns(wide, band, count):
    rows = count * ROWS
    lhs = wide[:, 0:rows, :].reshape(BLOCKS * rows, 256)
    return jnp.dot(lhs, band[...], preferred_element_type=jnp.float32).reshape(BLOCKS, rows, 256)


def joined(sums, g, p):
    lane = lax.broadcasted_iota(jnp.int32, (ROWS, 128), 1)
    rows = slice(p * ROWS, (p + 1) * ROWS)
    zero = jnp.zeros((ROWS, 128), jnp.float32)
    before = sums[g - 1, rows, 128:256] if g > 0 else zero
    after = sums[g + 1, rows, 128:256] if g < BLOCKS - 1 else zero
    return sums[g, rows, 0:128] + jnp.where(lane < 64, before, after)


def power(ext, out, prod, wide, band):
    for g in range(BLOCKS):
        prod[0, g] = ext[0, g] * ext[0, g] + ext[1, g] * ext[1, g]
    widen(prod, wide, 1)
    sums = columns(wide, band, 1)
    for g in range(BLOCKS):
        out[g] = joined(sums, g, 0)


def coherence(a_ext, pow_a, b_ext, pow_b, out_re, out_im, prod, wide, band):
    for g in range(BLOCKS):
        a_re, a_im = a_ext[0, g], a_ext[1, g]
        b_re, b_im = b_ext[0, g], b_ext[1, g]
        prod[0, g] = a_re * b_re + a_im * b_im
        prod[1, g] = a_im * b_re - a_re * b_im
    widen(prod, wide, 2)
    sums = columns(wide, band, 2)
    for g in range(BLOCKS):
        scale = lax.rsqrt(pow_a[g] * pow_b[g] + 1e-06)
        for p, out in ((0, out_re), (1, out_im)):
            out[:, 128 * g : 128 * g + 128] = joined(sums, g, p) * scale


CHIPS = 8


def spread_kernel(
    dates_hbm,
    offsets_hbm,
    re_hbm,
    im_hbm,
    refs,
    ref_edges,
    left,
    right,
    b_ext,
    pow_b,
    dates_ref,
    offsets_ref,
    re_ref,
    im_ref,
    band,
    prod,
    wide,
    load_sems,
    own_edges,
    packed,
    outward,
    halves,
    first_half,
    merged,
    pieces,
    pair_send,
    pair_recv,
    edge_send,
    edge_recv,
    first_send,
    first_recv,
    gather_send,
    gather_recv,
    spread_send,
    spread_recv,
    inward_send,
    inward_recv,
    rim_send,
    rim_recv,
    rim_in_send,
    rim_in_recv,
):
    me = lax.axis_index("date")
    tile = lax.axis_index("tile")
    chip, core = me // 2, me % 2
    tiles = lax.axis_size("tile")
    next_tile = {"tile": lax.rem(tile + 1, tiles)}
    last_tile = {"tile": lax.rem(tile + tiles - 1, tiles)}
    sibling = {"date": chip * 2 + 1 - core}

    def same_core(k):
        return {"date": k * 2 + core}

    def other(i):
        return lax.rem(chip + i, CHIPS)

    def remote(source, target, send, recv, to):
        return pltpu.make_async_remote_copy(src_ref=source, dst_ref=target, send_sem=send, recv_sem=recv, device_id=to, device_id_type=MESH)

    sources = ((dates_hbm, dates_ref), (offsets_hbm, offsets_ref), (re_hbm, re_ref), (im_hbm, im_ref))
    loads = [pltpu.make_async_copy(a, b, load_sems.at[k]) for k, (a, b) in enumerate(sources)]
    for c in loads:
        c.start()

    barrier = pltpu.get_barrier_semaphore()

    def greet(target):
        pl.semaphore_signal(barrier, inc=1, device_id=target, device_id_type=MESH)

    @pl.loop(1, CHIPS)
    def _(i):
        greet(same_core(other(i)))

    greet(next_tile)
    greet(last_tile)
    greet(sibling)
    band[...] = band_matrix()

    for c in loads:
        c.wait()

    def half(slot, c):
        rows = pl.ds(pl.multiple_of(c * 32, 32), 32)
        return re_ref[slot, rows].reshape(4, 8, COLS), im_ref[slot, rows].reshape(4, 8, COLS)

    for s in range(1, REFS):
        slot = lax.rem(dates_ref[s], DATE_DEV)
        halves[core, s - 1, 0:4], halves[core, s - 1, 4:8] = half(slot, core)
        outward[s - 1, 0:4], outward[s - 1, 4:8] = half(slot, 1 - core)

    @pl.when(me == 0)
    def _():
        first_half[0:4], first_half[4:8] = half(0, 0)
        outward[REFS - 1, 0:4], outward[REFS - 1, 4:8] = half(0, 1)

    for j in range(DATE_DEV):
        own_edges[j, 0:2] = re_ref[j, 0:2]
        own_edges[j, 2:4] = re_ref[j, ROWS - 2 : ROWS]
        own_edges[j, 4:6] = im_ref[j, 0:2]
        own_edges[j, 6:8] = im_ref[j, ROWS - 2 : ROWS]

    pl.semaphore_wait(barrier, 10)

    to_sibling = remote(outward.at[pl.ds(0, 2)], halves.at[core], pair_send.at[0], pair_recv.at[0], sibling)
    first_to_sibling = remote(outward.at[REFS - 1], first_half, pair_send.at[1], pair_recv.at[1], sibling)
    to_sibling.start()

    def first_out(k):
        return remote(first_half.at[k], refs.at[0, core, k], first_send.at[k], first_recv.at[0], same_core(k))

    def first_all():
        refs[0, core, 0] = first_half[0]

        @pl.loop(1, CHIPS)
        def _(k):
            first_out(k).start()

    @pl.when(me == 0)
    def _():
        first_to_sibling.start()
        first_all()

    to_right = remote(own_edges, left, edge_send.at[0], edge_recv.at[0], next_tile)
    to_left = remote(own_edges, right, edge_send.at[1], edge_recv.at[1], last_tile)
    to_right.start()
    to_left.start()

    to_sibling.wait_recv()
    for s in range(1, REFS):
        owner_core = lax.rem(dates_ref[s] // DATE_DEV, 2)
        merged[:, s - 1] = halves[owner_core, s - 1]

    def gather(k):
        return remote(merged.at[k], pieces.at[chip], gather_send.at[k], gather_recv.at[chip], same_core(k))

    def gathered(k):
        return remote(merged.at[k], pieces.at[k], gather_send.at[k], gather_recv.at[k], same_core(k))

    @pl.loop(1, CHIPS)
    def _(i):
        gather(other(i)).start()

    @pl.when(me == 1)
    def _():
        first_to_sibling.wait_recv()
        first_all()

    def part(n, k):
        return refs.at[0, core, k] if n == 0 else refs.at[pl.ds(1, 2), core, k]

    def spread_out(n, k):
        return remote(part(n, chip), part(n, chip), spread_send.at[n, k], spread_recv.at[n, chip], same_core(k))

    def spread_in(n, k):
        return remote(part(n, k), part(n, k), spread_send.at[n, k], spread_recv.at[n, k], same_core(k))

    def inward(n, k):
        return remote(part(n, k), part(n, k), inward_send.at[n, k], inward_recv.at[n, k], sibling)

    def inward_in(n, k):
        there = refs.at[0, 1 - core, k] if n == 0 else refs.at[pl.ds(1, 2), 1 - core, k]
        return remote(there, there, inward_send.at[n, k], inward_recv.at[n, k], sibling)

    def spread_all(n):
        @pl.loop(1, CHIPS)
        def _(i):
            spread_out(n, other(i)).start()

        inward(n, chip).start()

    @pl.when(chip > 0)
    def _():
        first_out(chip).wait_recv()

    spread_all(0)
    pieces[chip] = merged[chip]

    to_right.wait()
    to_left.wait()
    has_top = (tile > 0).astype(jnp.float32)
    has_bottom = (tile < tiles - 1).astype(jnp.float32)

    @pl.loop(0, DATE_DEV)
    def _(j):
        offset = offsets_ref[me * DATE_DEV + j]

        def shifted(x):
            for step in (1, 2, 4):
                x = jnp.where(lax.rem(offset // step, 2) == 1, pltpu.roll(x, COLS - step, 1), x)
            column = lax.broadcasted_iota(jnp.int32, x.shape, 1)
            return jnp.where(column < COLS - offset, x, 0.0)

        above_rows = shifted(left[j]) * has_top
        below_rows = shifted(right[j]) * has_bottom
        lay(b_ext.at[j], 0, shifted(re_ref[j]), above_rows[2:4], below_rows[0:2])
        lay(b_ext.at[j], 1, shifted(im_ref[j]), above_rows[6:8], below_rows[4:6])
        power(b_ext.at[j], pow_b.at[j], prod, wide, band)

    @pl.loop(1, CHIPS)
    def _(i):
        gathered(other(i)).wait_recv()

    for s in range(1, REFS):
        refs[s, core, chip] = pieces[dates_ref[s] // (2 * DATE_DEV), s - 1]

    below = (core == 0) & (lax.rem(chip, 4) == 0)
    above = (core == 1) & (lax.rem(chip, 4) == 3)
    own_kind = jnp.where(core == 0, 0, 2) + chip // 4

    def rim_over(to):
        return remote(packed, ref_edges.at[own_kind], rim_send.at[0], rim_recv.at[4], to)

    @pl.when(below)
    def _():
        for s in range(REFS):
            packed[2 * s : 2 * s + 2] = refs[s, core, chip, 0:2]
        packed[6:8] = jnp.zeros((2, COLS), jnp.float32)
        rim_over(last_tile).start()

    @pl.when(above)
    def _():
        for s in range(REFS):
            packed[2 * s : 2 * s + 2] = refs[s, core, chip, 6:8]
        packed[6:8] = jnp.zeros((2, COLS), jnp.float32)
        rim_over(next_tile).start()

    spread_all(1)

    def rim_out(k):
        return remote(ref_edges.at[own_kind], ref_edges.at[own_kind], rim_send.at[1 + k], rim_recv.at[own_kind], same_core(k))

    def rim_in(kind):
        return remote(ref_edges.at[kind], ref_edges.at[kind], rim_send.at[0], rim_recv.at[kind], sibling)

    def rim_inward(kind):
        return remote(ref_edges.at[kind], ref_edges.at[kind], rim_in_send.at[kind], rim_in_recv.at[kind], sibling)

    @pl.when(below | above)
    def _():
        rim_over(next_tile).wait_recv()

        @pl.loop(1, CHIPS)
        def _(i):
            rim_out(other(i)).start()

        rim_inward(own_kind).start()

    for n in range(2):

        @pl.loop(1, CHIPS)
        def _(i):
            k = other(i)
            spread_in(n, k).wait_recv()
            inward(n, k).start()

    @pl.loop(0, 2)
    def _(m):
        kind = core * 2 + m

        @pl.when(jnp.logical_not((below | above) & (kind == own_kind)))
        def _():
            rim_in(kind).wait_recv()
            rim_inward(kind).start()

    for n in range(2):

        @pl.loop(0, CHIPS)
        def _(k):
            inward_in(n, k).wait_recv()

    @pl.loop(0, 2)
    def _(m):
        rim_inward((1 - core) * 2 + m).wait_recv()
        rim_inward(core * 2 + m).wait_send()

    to_sibling.wait_send()

    @pl.when(me == 0)
    def _():
        first_to_sibling.wait_send()

    @pl.when(chip == 0)
    def _():
        @pl.loop(1, CHIPS)
        def _(k):
            first_out(k).wait_send()

    @pl.when(below | above)
    def _():
        rim_over(next_tile).wait_send()

        @pl.loop(1, CHIPS)
        def _(i):
            rim_out(other(i)).wait_send()

    @pl.loop(1, CHIPS)
    def _(i):
        gather(other(i)).wait_send()

    for n in range(2):

        @pl.loop(1, CHIPS)
        def _(i):
            spread_out(n, other(i)).wait_send()
            inward(n, other(i)).wait_send()

        inward(n, chip).wait_send()


def spread(dates, offsets, slc_re, slc_im):
    vmem = pl.BlockSpec(memory_space=pltpu.VMEM)
    hbm = pl.BlockSpec(memory_space=pltpu.HBM)
    dates_all = offsets.shape[0]
    f32 = jnp.float32
    dma = pltpu.SemaphoreType.DMA
    return pl.pallas_call(
        spread_kernel,
        out_shape=(
            jax.ShapeDtypeStruct((REFS, 2, CHIPS, 8, COLS), f32),
            jax.ShapeDtypeStruct((4, 8, COLS), f32),
            jax.ShapeDtypeStruct((DATE_DEV, 8, COLS), f32),
            jax.ShapeDtypeStruct((DATE_DEV, 8, COLS), f32),
            jax.ShapeDtypeStruct((DATE_DEV, 2, BLOCKS, 72, 128), f32),
            jax.ShapeDtypeStruct((DATE_DEV, BLOCKS, ROWS, 128), f32),
        ),
        in_specs=[hbm] * 4,
        out_specs=(vmem,) * 6,
        scratch_shapes=[
            pltpu.SMEM((STEPS,), jnp.int32),
            pltpu.SMEM((dates_all,), jnp.int32),
            pltpu.VMEM((DATE_DEV, ROWS, COLS), f32),
            pltpu.VMEM((DATE_DEV, ROWS, COLS), f32),
            pltpu.VMEM((256, 256), jnp.bfloat16),
            pltpu.VMEM((2, BLOCKS, 72, 128), f32),
            pltpu.VMEM((BLOCKS, 2 * ROWS, 256), jnp.bfloat16),
            dma((4,)),
            pltpu.VMEM((DATE_DEV, 8, COLS), f32),
            pltpu.VMEM((8, COLS), f32),
            pltpu.VMEM((REFS, CHIPS, 8, COLS), f32),
            pltpu.VMEM((2, 2, CHIPS, 8, COLS), f32),
            pltpu.VMEM((CHIPS, 8, COLS), f32),
            pltpu.VMEM((CHIPS, 2, 8, COLS), f32),
            pltpu.VMEM((CHIPS, 2, 8, COLS), f32),
            dma((2,)),
            dma((2,)),
            dma((2,)),
            dma((2,)),
            dma((CHIPS,)),
            dma((1,)),
            dma((CHIPS,)),
            dma((CHIPS,)),
            dma((2, CHIPS)),
            dma((2, CHIPS)),
            dma((2, CHIPS)),
            dma((2, CHIPS)),
            dma((CHIPS + 1,)),
            dma((5,)),
            dma((4,)),
            dma((4,)),
        ],
        compiler_params=pltpu.CompilerParams(collective_id=0, has_side_effects=True, vmem_limit_bytes=VMEM_LIMIT),
        name="spread",
    )(dates, offsets, slc_re, slc_im)


def compute_kernel(
    dates_hbm,
    keep_hbm,
    re_hbm,
    im_hbm,
    left,
    right,
    refs,
    ref_edges,
    b_ext,
    pow_b,
    out_re,
    out_im,
    dates_ref,
    keep_ref,
    band,
    own,
    zeros,
    stage,
    a_ext,
    prod,
    wide,
    pow_a,
    own_sems,
    out_sems,
):
    me = lax.axis_index("date")
    tile = lax.axis_index("tile")
    has_top = (tile > 0).astype(jnp.float32)
    has_bottom = (tile < lax.axis_size("tile") - 1).astype(jnp.float32)
    outs = (out_re, out_im)

    def zero_out(s, j, p):
        return pltpu.make_async_copy(zeros, outs[p].at[s, j], out_sems.at[p, s, j])

    def value_out(s, j, p):
        return pltpu.make_async_copy(stage.at[p, s, j], outs[p].at[s, j], out_sems.at[p, s, j])

    def valid(s, j):
        date = me * DATE_DEV + j
        return (keep_ref[s, date] == 1) & (date > dates_ref[s])

    scalars = ((dates_hbm, dates_ref), (keep_hbm, keep_ref))
    loads = [pltpu.make_async_copy(a, b, own_sems.at[2 + k]) for k, (a, b) in enumerate(scalars)]
    for c in loads:
        c.start()
    zeros[...] = jnp.zeros_like(zeros)
    band[...] = band_matrix()
    for c in loads:
        c.wait()

    @pl.loop(0, STEPS)
    def _(s):
        @pl.loop(0, DATE_DEV)
        def _(j):
            @pl.when(jnp.logical_not(valid(s, j)))
            def _():
                zero_out(s, j, 0).start()
                zero_out(s, j, 1).start()

    def edge_rows(tile_rows, at):
        return jnp.where(at == 0, tile_rows[0:2], jnp.where(at == 1, tile_rows[2:4], tile_rows[4:6]))

    @pl.loop(0, STEPS)
    def _(s):
        some = valid(s, 0) | valid(s, 1) | valid(s, 2) | valid(s, 3)

        @pl.when(some & (s < REFS))
        def _():
            at = jnp.minimum(s, REFS - 1)
            for p in range(2):
                rows = refs[at, :, 4 * p : 4 * p + 4].reshape(ROWS, COLS)
                top = edge_rows(ref_edges[2 + p], at) * has_top
                bottom = edge_rows(ref_edges[p], at) * has_bottom
                lay(a_ext, p, rows, top, bottom)

        @pl.when(some & (s == REFS))
        def _():
            slot = DATE_DEV - 2
            loads = [pltpu.make_async_copy(h.at[slot], own.at[p], own_sems.at[p]) for p, h in enumerate((re_hbm, im_hbm))]
            for c in loads:
                c.start()
            for c in loads:
                c.wait()
            for p in range(2):
                top = left[slot, 4 * p + 2 : 4 * p + 4] * has_top
                bottom = right[slot, 4 * p : 4 * p + 2] * has_bottom
                lay(a_ext, p, own[p], top, bottom)

        @pl.when(some)
        def _():
            power(a_ext, pow_a, prod, wide, band)

        @pl.loop(0, DATE_DEV)
        def _(j):
            @pl.when(valid(s, j))
            def _():
                coherence(a_ext, pow_a, b_ext.at[j], pow_b.at[j], stage.at[0, s, j], stage.at[1, s, j], prod, wide, band)
                value_out(s, j, 0).start()
                value_out(s, j, 1).start()

    @pl.loop(0, STEPS)
    def _(s):
        @pl.loop(0, DATE_DEV)
        def _(j):
            value_out(s, j, 0).wait()
            value_out(s, j, 1).wait()


def compute(dates, keep, slc_re, slc_im, left, right, refs, ref_edges, b_ext, pow_b):
    vmem = pl.BlockSpec(memory_space=pltpu.VMEM)
    hbm = pl.BlockSpec(memory_space=pltpu.HBM)
    shape = jax.ShapeDtypeStruct((STEPS, DATE_DEV, ROWS, COLS), jnp.float32)
    f32 = jnp.float32
    return pl.pallas_call(
        compute_kernel,
        out_shape=(shape, shape),
        in_specs=[hbm] * 4 + [vmem] * 6,
        out_specs=(hbm, hbm),
        scratch_shapes=[
            pltpu.SMEM((STEPS,), jnp.int32),
            pltpu.SMEM(keep.shape, jnp.int32),
            pltpu.VMEM((256, 256), jnp.bfloat16),
            pltpu.VMEM((2, ROWS, COLS), f32),
            pltpu.VMEM((ROWS, COLS), f32),
            pltpu.VMEM((2, STEPS, DATE_DEV, ROWS, COLS), f32),
            pltpu.VMEM((2, BLOCKS, 72, 128), f32),
            pltpu.VMEM((2, BLOCKS, 72, 128), f32),
            pltpu.VMEM((BLOCKS, 2 * ROWS, 256), jnp.bfloat16),
            pltpu.VMEM((BLOCKS, ROWS, 128), f32),
            pltpu.SemaphoreType.DMA((4,)),
            pltpu.SemaphoreType.DMA((2, STEPS, DATE_DEV)),
        ],
        compiler_params=pltpu.CompilerParams(vmem_limit_bytes=VMEM_LIMIT),
        name="coherence",
    )(dates, keep, slc_re, slc_im, left, right, refs, ref_edges, b_ext, pow_b)


def body(slc_re, slc_im, ref_dates, pair_keep, col_offsets):
    hbm = [pltpu.with_memory_space_constraint(x, pltpu.HBM) for x in (slc_re, slc_im, ref_dates, pair_keep, col_offsets)]
    slc_re, slc_im, ref_dates, pair_keep, col_offsets = hbm
    refs, ref_edges, left, right, b_ext, pow_b = spread(ref_dates, col_offsets, slc_re, slc_im)
    return compute(ref_dates, pair_keep, slc_re, slc_im, left, right, refs, ref_edges, b_ext, pow_b)


def solution(mesh):
    placed = (P("date", "tile", None), P("date", "tile", None), P(), P(), P())
    return jax.shard_map(
        body,
        mesh=mesh,
        in_specs=placed,
        out_specs=(P(None, "date", "tile", None), P(None, "date", "tile", None)),
        check_vma=False,
    )
```

```python
import jax
import jax.numpy as jnp
from jax import lax
from jax.experimental import pallas as pl
from jax.experimental.pallas import tpu as pltpu
from jax.sharding import PartitionSpec as P

MESH = pl.DeviceIdType.MESH
DATE_DEV = 4
ROWS = 64
COLS = 1024
BLOCKS = COLS // 128
REFS = 3
STEPS = 4
VMEM_LIMIT = 24 * 2**20


def band_matrix():
    k = lax.rem(lax.broadcasted_iota(jnp.int32, (256, 256), 0), 128)
    c = lax.broadcasted_iota(jnp.int32, (256, 256), 1)
    within = (c < 128) & (k >= c - 10) & (k <= c + 9)
    after = (c >= 128) & (c < 138) & (k >= c - 10)
    before = (c >= 247) & (k <= c - 247)
    return jnp.where(within | after | before, 1.0, 0.0).astype(jnp.bfloat16)


def lay(ext, plane, rows, top, bottom):
    for g in range(BLOCKS):
        cut = slice(128 * g, 128 * g + 128)
        ext[plane, g, 0:2] = top[:, cut]
        ext[plane, g, 2 : ROWS + 2] = rows[:, cut]
        ext[plane, g, ROWS + 2 : ROWS + 4] = bottom[:, cut]


def widen(prod, wide, count):
    for g in range(BLOCKS):
        for p in range(count):
            total = prod[p, g, 0:ROWS]
            for k in range(1, 5):
                total = total + prod[p, g, k : k + ROWS]
            high = total.astype(jnp.bfloat16)
            low = (total - high.astype(jnp.float32)).astype(jnp.bfloat16)
            wide[g, p * ROWS : (p + 1) * ROWS, 0:128] = high
            wide[g, p * ROWS : (p + 1) * ROWS, 128:256] = low


def columns(wide, band, count):
    rows = count * ROWS
    lhs = wide[:, 0:rows, :].reshape(BLOCKS * rows, 256)
    return jnp.dot(lhs, band[...], preferred_element_type=jnp.float32).reshape(BLOCKS, rows, 256)


def joined(sums, g, p):
    lane = lax.broadcasted_iota(jnp.int32, (ROWS, 128), 1)
    rows = slice(p * ROWS, (p + 1) * ROWS)
    zero = jnp.zeros((ROWS, 128), jnp.float32)
    before = sums[g - 1, rows, 128:256] if g > 0 else zero
    after = sums[g + 1, rows, 128:256] if g < BLOCKS - 1 else zero
    return sums[g, rows, 0:128] + jnp.where(lane < 64, before, after)


def power(ext, out, prod, wide, band):
    for g in range(BLOCKS):
        prod[0, g] = ext[0, g] * ext[0, g] + ext[1, g] * ext[1, g]
    widen(prod, wide, 1)
    sums = columns(wide, band, 1)
    for g in range(BLOCKS):
        out[g] = joined(sums, g, 0)


def coherence(a_ext, pow_a, b_ext, pow_b, out_re, out_im, prod, wide, band):
    for g in range(BLOCKS):
        a_re, a_im = a_ext[0, g], a_ext[1, g]
        b_re, b_im = b_ext[0, g], b_ext[1, g]
        prod[0, g] = a_re * b_re + a_im * b_im
        prod[1, g] = a_im * b_re - a_re * b_im
    widen(prod, wide, 2)
    sums = columns(wide, band, 2)
    for g in range(BLOCKS):
        scale = lax.rsqrt(pow_a[g] * pow_b[g] + 1e-06)
        for p, out in ((0, out_re), (1, out_im)):
            out[:, 128 * g : 128 * g + 128] = joined(sums, g, p) * scale


CHIPS = 8


def spread_kernel(
    dates_hbm,
    offsets_hbm,
    re_hbm,
    im_hbm,
    refs,
    ref_edges,
    left,
    right,
    b_ext,
    pow_b,
    first_re,
    first_im,
    dates_ref,
    offsets_ref,
    re_ref,
    im_ref,
    band,
    prod,
    wide,
    a_ext,
    pow_a,
    load_sems,
    first_edges,
    own_edges,
    packed,
    outward,
    second_halves,
    third_halves,
    first_half,
    merged,
    second_pieces,
    third_pieces,
    pair_send,
    pair_recv,
    edge_send,
    edge_recv,
    first_send,
    first_recv,
    gather_send,
    gather_recv,
    spread_send,
    spread_recv,
    inward_send,
    inward_recv,
    rim_send,
    rim_recv,
    rim_in_send,
    rim_in_recv,
    top_send,
    top_recv,
):
    me = lax.axis_index("date")
    tile = lax.axis_index("tile")
    chip, core = me // 2, me % 2
    halves = (second_halves, third_halves)
    pieces = (second_pieces, third_pieces)
    tiles = lax.axis_size("tile")
    next_tile = {"tile": lax.rem(tile + 1, tiles)}
    last_tile = {"tile": lax.rem(tile + tiles - 1, tiles)}
    sibling = {"date": chip * 2 + 1 - core}

    def same_core(k):
        return {"date": k * 2 + core}

    def other(i):
        return lax.rem(chip + i, CHIPS)

    def remote(source, target, send, recv, to):
        return pltpu.make_async_remote_copy(src_ref=source, dst_ref=target, send_sem=send, recv_sem=recv, device_id=to, device_id_type=MESH)

    sources = ((dates_hbm, dates_ref), (offsets_hbm, offsets_ref), (re_hbm, re_ref), (im_hbm, im_ref))
    loads = [pltpu.make_async_copy(a, b, load_sems.at[k]) for k, (a, b) in enumerate(sources)]
    for c in loads:
        c.start()

    barrier = pltpu.get_barrier_semaphore()

    def greet(target):
        pl.semaphore_signal(barrier, inc=1, device_id=target, device_id_type=MESH)

    @pl.loop(1, CHIPS)
    def _(i):
        greet(same_core(other(i)))

    greet(next_tile)
    greet(last_tile)
    greet(sibling)
    band[...] = band_matrix()

    for c in loads:
        c.wait()

    def half(slot, c):
        rows = pl.ds(pl.multiple_of(c * 32, 32), 32)
        return re_ref[slot, rows].reshape(4, 8, COLS), im_ref[slot, rows].reshape(4, 8, COLS)

    for s in range(1, REFS):
        slot = lax.rem(dates_ref[s], DATE_DEV)
        halves[s - 1][core, 0:4], halves[s - 1][core, 4:8] = half(slot, core)
        outward[s - 1, 0:4], outward[s - 1, 4:8] = half(slot, 1 - core)

    @pl.when(me == 0)
    def _():
        first_half[0:4], first_half[4:8] = half(0, 0)
        outward[REFS - 1, 0:4], outward[REFS - 1, 4:8] = half(0, 1)

    for j in range(DATE_DEV):
        own_edges[j, 0:2] = re_ref[j, 0:2]
        own_edges[j, 2:4] = re_ref[j, ROWS - 2 : ROWS]
        own_edges[j, 4:6] = im_ref[j, 0:2]
        own_edges[j, 6:8] = im_ref[j, ROWS - 2 : ROWS]

    pl.semaphore_wait(barrier, 10)

    def to_sibling(n):
        return remote(outward.at[n], halves[n].at[core], pair_send.at[n], pair_recv.at[n], sibling)

    first_to_sibling = remote(outward.at[REFS - 1], first_half, pair_send.at[2], pair_recv.at[2], sibling)
    to_sibling(0).start()

    def first_out(k):
        return remote(first_half.at[k], refs.at[0, core, k], first_send.at[k], first_recv.at[0], same_core(k))

    def first_all():
        refs[0, core, 0] = first_half[0]

        @pl.loop(1, CHIPS)
        def _(k):
            first_out(k).start()

    @pl.when(me == 0)
    def _():
        first_to_sibling.start()
        first_all()

    to_right = remote(own_edges, left, edge_send.at[0], edge_recv.at[0], next_tile)
    to_left = remote(own_edges, right, edge_send.at[1], edge_recv.at[1], last_tile)
    to_sibling(1).start()
    to_right.start()
    to_left.start()

    def gather(n, k):
        return remote(merged.at[n, k], pieces[n].at[chip], gather_send.at[n, k], gather_recv.at[n, chip], same_core(k))

    def gathered(n, k):
        return remote(merged.at[n, k], pieces[n].at[k], gather_send.at[n, k], gather_recv.at[n, k], same_core(k))

    @pl.when(me == 1)
    def _():
        first_to_sibling.wait_recv()
        first_all()

    for n in range(2):
        to_sibling(n).wait_recv()
        owner_core = lax.rem(dates_ref[n + 1] // DATE_DEV, 2)
        merged[n] = halves[n][owner_core]

        @pl.loop(1, CHIPS)
        def _(i):
            gather(n, other(i)).start()

        pieces[n][chip] = merged[n, chip]

    def part(n, k):
        return refs.at[n, core, k]

    def spread_out(n, k):
        return remote(part(n, chip), part(n, chip), spread_send.at[n, k], spread_recv.at[n, chip], same_core(k))

    def spread_in(n, k):
        return remote(part(n, k), part(n, k), spread_send.at[n, k], spread_recv.at[n, k], same_core(k))

    def inward(n, k):
        return remote(part(n, k), part(n, k), inward_send.at[n, k], inward_recv.at[n, k], sibling)

    def inward_in(n, k):
        there = refs.at[n, 1 - core, k]
        return remote(there, there, inward_send.at[n, k], inward_recv.at[n, k], sibling)

    def spread_all(n):
        @pl.loop(1, CHIPS)
        def _(i):
            spread_out(n, other(i)).start()

        inward(n, chip).start()

    @pl.when(chip > 0)
    def _():
        first_out(chip).wait_recv()

    spread_all(0)

    to_right.wait()
    to_left.wait()
    has_top = (tile > 0).astype(jnp.float32)
    has_bottom = (tile < tiles - 1).astype(jnp.float32)

    def first_edges_out(k, to):
        return remote(first_edges, first_edges, top_send.at[k], top_recv.at[0], to)

    @pl.when(me == 0)
    def _():
        first_edges[0:2] = left[0, 2:4]
        first_edges[2:4] = left[0, 6:8]
        first_edges[4:6] = right[0, 0:2]
        first_edges[6:8] = right[0, 4:6]

        @pl.loop(1, CHIPS)
        def _(k):
            first_edges_out(k, same_core(k)).start()

        first_edges_out(0, sibling).start()

    def take(n):
        @pl.loop(1, CHIPS)
        def _(i):
            gathered(n, other(i)).wait_recv()

        refs[n + 1, core, chip] = pieces[n][dates_ref[n + 1] // (2 * DATE_DEV)]

    take(0)
    spread_all(1)
    take(1)

    below = (core == 0) & (lax.rem(chip, 4) == 0)
    above = (core == 1) & (lax.rem(chip, 4) == 3)
    own_kind = jnp.where(core == 0, 0, 2) + chip // 4

    def rim_over(to):
        return remote(packed, ref_edges.at[own_kind], rim_send.at[0], rim_recv.at[4], to)

    @pl.when(below)
    def _():
        for s in range(REFS):
            packed[2 * s : 2 * s + 2] = refs[s, core, chip, 0:2]
        packed[6:8] = jnp.zeros((2, COLS), jnp.float32)
        rim_over(last_tile).start()

    @pl.when(above)
    def _():
        for s in range(REFS):
            packed[2 * s : 2 * s + 2] = refs[s, core, chip, 6:8]
        packed[6:8] = jnp.zeros((2, COLS), jnp.float32)
        rim_over(next_tile).start()

    spread_all(2)

    def rim_out(k):
        return remote(ref_edges.at[own_kind], ref_edges.at[own_kind], rim_send.at[1 + k], rim_recv.at[own_kind], same_core(k))

    def rim_in(kind):
        return remote(ref_edges.at[kind], ref_edges.at[kind], rim_send.at[0], rim_recv.at[kind], sibling)

    def rim_inward(kind):
        return remote(ref_edges.at[kind], ref_edges.at[kind], rim_in_send.at[kind], rim_in_recv.at[kind], sibling)

    def pass_on(n):
        @pl.loop(1, CHIPS)
        def _(i):
            k = other(i)
            spread_in(n, k).wait_recv()
            inward(n, k).start()

    def passed_on(n):
        @pl.loop(0, CHIPS)
        def _(k):
            inward_in(n, k).wait_recv()

    @pl.when(me > 0)
    def _():
        first_edges_out(0, sibling).wait_recv()

    @pl.when((me > 0) & (core == 0))
    def _():
        first_edges_out(0, sibling).start()

    @pl.when(below | above)
    def _():
        rim_over(next_tile).wait_recv()

        @pl.loop(1, CHIPS)
        def _(i):
            rim_out(other(i)).start()

        rim_inward(own_kind).start()

    pass_on(0)

    @pl.loop(0, DATE_DEV)
    def _(j):
        offset = offsets_ref[me * DATE_DEV + j]

        def shifted(x):
            for step in (1, 2, 4):
                x = jnp.where(lax.rem(offset // step, 2) == 1, pltpu.roll(x, COLS - step, 1), x)
            column = lax.broadcasted_iota(jnp.int32, x.shape, 1)
            return jnp.where(column < COLS - offset, x, 0.0)

        above_rows = shifted(left[j]) * has_top
        below_rows = shifted(right[j]) * has_bottom
        lay(b_ext.at[j], 0, shifted(re_ref[j]), above_rows[2:4], below_rows[0:2])
        lay(b_ext.at[j], 1, shifted(im_ref[j]), above_rows[6:8], below_rows[4:6])
        power(b_ext.at[j], pow_b.at[j], prod, wide, band)

    passed_on(0)
    for p in range(2):
        rows = refs[0, :, 4 * p : 4 * p + 4].reshape(ROWS, COLS)
        top = first_edges[2 * p : 2 * p + 2] * has_top
        bottom = first_edges[2 * p + 4 : 2 * p + 6] * has_bottom
        lay(a_ext, p, rows, top, bottom)
    power(a_ext, pow_a, prod, wide, band)

    @pl.loop(0, DATE_DEV)
    def _(j):
        coherence(a_ext, pow_a, b_ext.at[j], pow_b.at[j], first_re.at[j], first_im.at[j], prod, wide, band)

    pass_on(1)

    @pl.loop(0, 2)
    def _(m):
        kind = core * 2 + m

        @pl.when(jnp.logical_not((below | above) & (kind == own_kind)))
        def _():
            rim_in(kind).wait_recv()
            rim_inward(kind).start()

    pass_on(2)
    passed_on(1)
    passed_on(2)

    @pl.loop(0, 2)
    def _(m):
        rim_inward((1 - core) * 2 + m).wait_recv()
        rim_inward(core * 2 + m).wait_send()

    to_sibling(0).wait_send()
    to_sibling(1).wait_send()

    @pl.when(core == 0)
    def _():
        first_edges_out(0, sibling).wait_send()

    @pl.when(me == 0)
    def _():
        first_to_sibling.wait_send()

        @pl.loop(1, CHIPS)
        def _(k):
            first_edges_out(k, same_core(k)).wait_send()

    @pl.when(chip == 0)
    def _():
        @pl.loop(1, CHIPS)
        def _(k):
            first_out(k).wait_send()

    @pl.when(below | above)
    def _():
        rim_over(next_tile).wait_send()

        @pl.loop(1, CHIPS)
        def _(i):
            rim_out(other(i)).wait_send()

    for n in range(2):

        @pl.loop(1, CHIPS)
        def _(i):
            gather(n, other(i)).wait_send()

    for n in range(REFS):

        @pl.loop(1, CHIPS)
        def _(i):
            spread_out(n, other(i)).wait_send()
            inward(n, other(i)).wait_send()

        inward(n, chip).wait_send()


def spread(dates, offsets, slc_re, slc_im):
    vmem = pl.BlockSpec(memory_space=pltpu.VMEM)
    hbm = pl.BlockSpec(memory_space=pltpu.HBM)
    dates_all = offsets.shape[0]
    f32 = jnp.float32
    dma = pltpu.SemaphoreType.DMA
    return pl.pallas_call(
        spread_kernel,
        out_shape=(
            jax.ShapeDtypeStruct((REFS, 2, CHIPS, 8, COLS), f32),
            jax.ShapeDtypeStruct((4, 8, COLS), f32),
            jax.ShapeDtypeStruct((DATE_DEV, 8, COLS), f32),
            jax.ShapeDtypeStruct((DATE_DEV, 8, COLS), f32),
            jax.ShapeDtypeStruct((DATE_DEV, 2, BLOCKS, 72, 128), f32),
            jax.ShapeDtypeStruct((DATE_DEV, BLOCKS, ROWS, 128), f32),
            jax.ShapeDtypeStruct((DATE_DEV, ROWS, COLS), f32),
            jax.ShapeDtypeStruct((DATE_DEV, ROWS, COLS), f32),
        ),
        in_specs=[hbm] * 4,
        out_specs=(vmem,) * 8,
        scratch_shapes=[
            pltpu.SMEM((STEPS,), jnp.int32),
            pltpu.SMEM((dates_all,), jnp.int32),
            pltpu.VMEM((DATE_DEV, ROWS, COLS), f32),
            pltpu.VMEM((DATE_DEV, ROWS, COLS), f32),
            pltpu.VMEM((256, 256), jnp.bfloat16),
            pltpu.VMEM((2, BLOCKS, 72, 128), f32),
            pltpu.VMEM((BLOCKS, 2 * ROWS, 256), jnp.bfloat16),
            pltpu.VMEM((2, BLOCKS, 72, 128), f32),
            pltpu.VMEM((BLOCKS, ROWS, 128), f32),
            dma((4,)),
            pltpu.VMEM((8, COLS), f32),
            pltpu.VMEM((DATE_DEV, 8, COLS), f32),
            pltpu.VMEM((8, COLS), f32),
            pltpu.VMEM((REFS, CHIPS, 8, COLS), f32),
            pltpu.VMEM((2, CHIPS, 8, COLS), f32),
            pltpu.VMEM((2, CHIPS, 8, COLS), f32),
            pltpu.VMEM((CHIPS, 8, COLS), f32),
            pltpu.VMEM((2, CHIPS, 8, COLS), f32),
            pltpu.VMEM((CHIPS, 8, COLS), f32),
            pltpu.VMEM((CHIPS, 8, COLS), f32),
            dma((3,)),
            dma((3,)),
            dma((2,)),
            dma((2,)),
            dma((CHIPS,)),
            dma((1,)),
            dma((2, CHIPS)),
            dma((2, CHIPS)),
            dma((REFS, CHIPS)),
            dma((REFS, CHIPS)),
            dma((REFS, CHIPS)),
            dma((REFS, CHIPS)),
            dma((CHIPS + 1,)),
            dma((5,)),
            dma((4,)),
            dma((4,)),
            dma((CHIPS,)),
            dma((1,)),
        ],
        compiler_params=pltpu.CompilerParams(collective_id=0, has_side_effects=True, vmem_limit_bytes=VMEM_LIMIT),
        name="spread",
    )(dates, offsets, slc_re, slc_im)


def compute_kernel(
    dates_hbm,
    keep_hbm,
    re_hbm,
    im_hbm,
    left,
    right,
    refs,
    ref_edges,
    b_ext,
    pow_b,
    first_re,
    first_im,
    out_re,
    out_im,
    dates_ref,
    keep_ref,
    band,
    own,
    zeros,
    stage,
    a_ext,
    prod,
    wide,
    pow_a,
    own_sems,
    out_sems,
):
    me = lax.axis_index("date")
    tile = lax.axis_index("tile")
    has_top = (tile > 0).astype(jnp.float32)
    has_bottom = (tile < lax.axis_size("tile") - 1).astype(jnp.float32)
    outs = (out_re, out_im)

    def zero_out(s, j, p):
        return pltpu.make_async_copy(zeros, outs[p].at[s, j], out_sems.at[p, s, j])

    def value_out(s, j, p):
        return pltpu.make_async_copy(stage.at[p, s - 1, j], outs[p].at[s, j], out_sems.at[p, s, j])

    def first_out(j, p):
        return pltpu.make_async_copy((first_re, first_im)[p].at[j], outs[p].at[0, j], out_sems.at[p, 0, j])

    slot = DATE_DEV - 2
    own_loads = [pltpu.make_async_copy(h.at[slot], own.at[p], own_sems.at[p]) for p, h in enumerate((re_hbm, im_hbm))]

    def valid(s, j):
        date = me * DATE_DEV + j
        return (keep_ref[s, date] == 1) & (date > dates_ref[s])

    scalars = ((dates_hbm, dates_ref), (keep_hbm, keep_ref))
    loads = [pltpu.make_async_copy(a, b, own_sems.at[2 + k]) for k, (a, b) in enumerate(scalars)]
    for c in loads:
        c.start()
    zeros[...] = jnp.zeros_like(zeros)
    band[...] = band_matrix()
    for c in loads:
        c.wait()

    @pl.loop(0, STEPS)
    def _(s):
        @pl.loop(0, DATE_DEV)
        def _(j):
            @pl.when(jnp.logical_not(valid(s, j)))
            def _():
                zero_out(s, j, 0).start()
                zero_out(s, j, 1).start()

    @pl.loop(0, DATE_DEV)
    def _(j):
        @pl.when(valid(0, j))
        def _():
            first_out(j, 0).start()
            first_out(j, 1).start()

    last = valid(REFS, DATE_DEV - 1)

    @pl.when(last)
    def _():
        for c in own_loads:
            c.start()

    def edge_rows(tile_rows, at):
        return jnp.where(at == 0, tile_rows[0:2], jnp.where(at == 1, tile_rows[2:4], tile_rows[4:6]))

    @pl.loop(1, STEPS)
    def _(s):
        some = valid(s, 0) | valid(s, 1) | valid(s, 2) | valid(s, 3)

        @pl.when(some & (s < REFS))
        def _():
            at = jnp.minimum(s, REFS - 1)
            for p in range(2):
                rows = refs[at, :, 4 * p : 4 * p + 4].reshape(ROWS, COLS)
                top = edge_rows(ref_edges[2 + p], at) * has_top
                bottom = edge_rows(ref_edges[p], at) * has_bottom
                lay(a_ext, p, rows, top, bottom)

        @pl.when(some & (s == REFS))
        def _():
            for c in own_loads:
                c.wait()
            for p in range(2):
                top = left[slot, 4 * p + 2 : 4 * p + 4] * has_top
                bottom = right[slot, 4 * p : 4 * p + 2] * has_bottom
                lay(a_ext, p, own[p], top, bottom)

        @pl.when(some)
        def _():
            power(a_ext, pow_a, prod, wide, band)

        @pl.loop(0, DATE_DEV)
        def _(j):
            @pl.when(valid(s, j))
            def _():
                coherence(a_ext, pow_a, b_ext.at[j], pow_b.at[j], stage.at[0, s - 1, j], stage.at[1, s - 1, j], prod, wide, band)
                value_out(s, j, 0).start()
                value_out(s, j, 1).start()

    @pl.loop(0, STEPS)
    def _(s):
        @pl.loop(0, DATE_DEV)
        def _(j):
            zero_out(s, j, 0).wait()
            zero_out(s, j, 1).wait()


def compute(dates, keep, slc_re, slc_im, *parts):
    vmem = pl.BlockSpec(memory_space=pltpu.VMEM)
    hbm = pl.BlockSpec(memory_space=pltpu.HBM)
    shape = jax.ShapeDtypeStruct((STEPS, DATE_DEV, ROWS, COLS), jnp.float32)
    f32 = jnp.float32
    return pl.pallas_call(
        compute_kernel,
        out_shape=(shape, shape),
        in_specs=[hbm] * 4 + [vmem] * len(parts),
        out_specs=(hbm, hbm),
        scratch_shapes=[
            pltpu.SMEM((STEPS,), jnp.int32),
            pltpu.SMEM(keep.shape, jnp.int32),
            pltpu.VMEM((256, 256), jnp.bfloat16),
            pltpu.VMEM((2, ROWS, COLS), f32),
            pltpu.VMEM((ROWS, COLS), f32),
            pltpu.VMEM((2, REFS, DATE_DEV, ROWS, COLS), f32),
            pltpu.VMEM((2, BLOCKS, 72, 128), f32),
            pltpu.VMEM((2, BLOCKS, 72, 128), f32),
            pltpu.VMEM((BLOCKS, 2 * ROWS, 256), jnp.bfloat16),
            pltpu.VMEM((BLOCKS, ROWS, 128), f32),
            pltpu.SemaphoreType.DMA((4,)),
            pltpu.SemaphoreType.DMA((2, STEPS, DATE_DEV)),
        ],
        compiler_params=pltpu.CompilerParams(vmem_limit_bytes=VMEM_LIMIT),
        name="coherence",
    )(dates, keep, slc_re, slc_im, *parts)


def body(slc_re, slc_im, ref_dates, pair_keep, col_offsets):
    hbm = [pltpu.with_memory_space_constraint(x, pltpu.HBM) for x in (slc_re, slc_im, ref_dates, pair_keep, col_offsets)]
    slc_re, slc_im, ref_dates, pair_keep, col_offsets = hbm
    parts = spread(ref_dates, col_offsets, slc_re, slc_im)
    order = (2, 3, 0, 1, 4, 5, 6, 7)
    return compute(ref_dates, pair_keep, slc_re, slc_im, *[parts[k] for k in order])


def solution(mesh):
    placed = (P("date", "tile", None), P("date", "tile", None), P(), P(), P())
    return jax.shard_map(
        body,
        mesh=mesh,
        in_specs=placed,
        out_specs=(P(None, "date", "tile", None), P(None, "date", "tile", None)),
        check_vma=False,
    )
```

```python
import jax
import jax.numpy as jnp
from jax import lax
from jax.experimental import pallas as pl
from jax.experimental.pallas import tpu as pltpu
from jax.sharding import PartitionSpec as P

MESH = pl.DeviceIdType.MESH
DATE_DEV = 4
ROWS = 64
COLS = 1024
BLOCKS = COLS // 128
REFS = 3
STEPS = 4
VMEM_LIMIT = 24 * 2**20


def band_matrix():
    k = lax.rem(lax.broadcasted_iota(jnp.int32, (256, 256), 0), 128)
    c = lax.broadcasted_iota(jnp.int32, (256, 256), 1)
    within = (c < 128) & (k >= c - 10) & (k <= c + 9)
    after = (c >= 128) & (c < 138) & (k >= c - 10)
    before = (c >= 247) & (k <= c - 247)
    return jnp.where(within | after | before, 1.0, 0.0).astype(jnp.bfloat16)


def lay(ext, plane, rows, top, bottom):
    for g in range(BLOCKS):
        cut = slice(128 * g, 128 * g + 128)
        ext[plane, g, 0:2] = top[:, cut]
        ext[plane, g, 2 : ROWS + 2] = rows[:, cut]
        ext[plane, g, ROWS + 2 : ROWS + 4] = bottom[:, cut]


def widen(prod, wide, count):
    for g in range(BLOCKS):
        for p in range(count):
            total = prod[p, g, 0:ROWS]
            for k in range(1, 5):
                total = total + prod[p, g, k : k + ROWS]
            high = total.astype(jnp.bfloat16)
            low = (total - high.astype(jnp.float32)).astype(jnp.bfloat16)
            wide[g, p * ROWS : (p + 1) * ROWS, 0:128] = high
            wide[g, p * ROWS : (p + 1) * ROWS, 128:256] = low


def columns(wide, band, count):
    rows = count * ROWS
    lhs = wide[:, 0:rows, :].reshape(BLOCKS * rows, 256)
    return jnp.dot(lhs, band[...], preferred_element_type=jnp.float32).reshape(BLOCKS, rows, 256)


def joined(sums, g, p):
    lane = lax.broadcasted_iota(jnp.int32, (ROWS, 128), 1)
    rows = slice(p * ROWS, (p + 1) * ROWS)
    zero = jnp.zeros((ROWS, 128), jnp.float32)
    before = sums[g - 1, rows, 128:256] if g > 0 else zero
    after = sums[g + 1, rows, 128:256] if g < BLOCKS - 1 else zero
    return sums[g, rows, 0:128] + jnp.where(lane < 64, before, after)


def power(ext, out, prod, wide, band):
    for g in range(BLOCKS):
        prod[0, g] = ext[0, g] * ext[0, g] + ext[1, g] * ext[1, g]
    widen(prod, wide, 1)
    sums = columns(wide, band, 1)
    for g in range(BLOCKS):
        out[g] = joined(sums, g, 0)


def coherence(a_ext, pow_a, b_ext, pow_b, out_re, out_im, prod, wide, band):
    for g in range(BLOCKS):
        a_re, a_im = a_ext[0, g], a_ext[1, g]
        b_re, b_im = b_ext[0, g], b_ext[1, g]
        prod[0, g] = a_re * b_re + a_im * b_im
        prod[1, g] = a_im * b_re - a_re * b_im
    widen(prod, wide, 2)
    sums = columns(wide, band, 2)
    for g in range(BLOCKS):
        scale = lax.rsqrt(pow_a[g] * pow_b[g] + 1e-06)
        for p, out in ((0, out_re), (1, out_im)):
            out[:, 128 * g : 128 * g + 128] = joined(sums, g, p) * scale


CHIPS = 8


def spread_kernel(
    dates_hbm,
    offsets_hbm,
    re_hbm,
    im_hbm,
    refs,
    ref_edges,
    left,
    right,
    b_ext,
    pow_b,
    first_re,
    first_im,
    dates_ref,
    offsets_ref,
    re_ref,
    im_ref,
    band,
    prod,
    wide,
    a_ext,
    pow_a,
    load_sems,
    first_edges,
    edges_right,
    edges_left,
    packed,
    outward,
    second_halves,
    third_halves,
    first_half,
    merged,
    second_pieces,
    third_pieces,
    pair_send,
    pair_recv,
    edge_send,
    edge_recv,
    first_send,
    first_recv,
    gather_send,
    gather_recv,
    spread_send,
    spread_recv,
    inward_send,
    inward_recv,
    rim_send,
    rim_recv,
    rim_in_send,
    rim_in_recv,
    top_send,
    top_recv,
):
    me = lax.axis_index("date")
    tile = lax.axis_index("tile")
    chip, core = me // 2, me % 2
    halves = (second_halves, third_halves)
    pieces = (second_pieces, third_pieces)
    tiles = lax.axis_size("tile")
    next_tile = {"tile": lax.rem(tile + 1, tiles)}
    last_tile = {"tile": lax.rem(tile + tiles - 1, tiles)}
    sibling = {"date": chip * 2 + 1 - core}

    def same_core(k):
        return {"date": k * 2 + core}

    def other(i):
        return lax.rem(chip + i, CHIPS)

    def remote(source, target, send, recv, to):
        return pltpu.make_async_remote_copy(src_ref=source, dst_ref=target, send_sem=send, recv_sem=recv, device_id=to, device_id_type=MESH)

    sources = ((dates_hbm, dates_ref), (offsets_hbm, offsets_ref), (re_hbm, re_ref), (im_hbm, im_ref))
    loads = [pltpu.make_async_copy(a, b, load_sems.at[k]) for k, (a, b) in enumerate(sources)]
    for c in loads:
        c.start()

    barrier = pltpu.get_barrier_semaphore()

    def greet(target):
        pl.semaphore_signal(barrier, inc=1, device_id=target, device_id_type=MESH)

    @pl.loop(1, CHIPS)
    def _(i):
        greet(same_core(other(i)))

    greet(next_tile)
    greet(last_tile)
    greet(sibling)
    band[...] = band_matrix()

    for c in loads:
        c.wait()

    def half(slot, c):
        rows = pl.ds(pl.multiple_of(c * 32, 32), 32)
        return re_ref[slot, rows].reshape(4, 8, COLS), im_ref[slot, rows].reshape(4, 8, COLS)

    for s in range(1, REFS):
        slot = lax.rem(dates_ref[s], DATE_DEV)
        halves[s - 1][core, 0:4], halves[s - 1][core, 4:8] = half(slot, core)
        outward[s - 1, 0:4], outward[s - 1, 4:8] = half(slot, 1 - core)

    @pl.when(me == 0)
    def _():
        first_half[0:4], first_half[4:8] = half(0, 0)
        outward[REFS - 1, 0:4], outward[REFS - 1, 4:8] = half(0, 1)

    for j in range(DATE_DEV):
        at = 4 * (j % 2)
        for p, plane in enumerate((re_ref, im_ref)):
            edges_right[j // 2, at + 2 * p : at + 2 * p + 2] = plane[j, ROWS - 2 : ROWS]
            edges_left[j // 2, at + 2 * p : at + 2 * p + 2] = plane[j, 0:2]

    pl.semaphore_wait(barrier, 10)

    def to_sibling(n):
        return remote(outward.at[n], halves[n].at[core], pair_send.at[n], pair_recv.at[n], sibling)

    first_to_sibling = remote(outward.at[REFS - 1], first_half, pair_send.at[2], pair_recv.at[2], sibling)
    to_sibling(0).start()
    to_right = remote(edges_right, left, edge_send.at[0], edge_recv.at[0], next_tile)
    to_left = remote(edges_left, right, edge_send.at[1], edge_recv.at[1], last_tile)
    to_right.start()
    to_left.start()

    def first_out(k):
        return remote(first_half.at[k], refs.at[0, core, k], first_send.at[k], first_recv.at[0], same_core(k))

    def first_all():
        refs[0, core, 0] = first_half[0]

        @pl.loop(1, CHIPS)
        def _(k):
            first_out(k).start()

    @pl.when(me == 0)
    def _():
        first_to_sibling.start()
        first_all()

    to_sibling(1).start()

    def gather(n, k):
        return remote(merged.at[n, k], pieces[n].at[chip], gather_send.at[n, k], gather_recv.at[n, chip], same_core(k))

    def gathered(n, k):
        return remote(merged.at[n, k], pieces[n].at[k], gather_send.at[n, k], gather_recv.at[n, k], same_core(k))

    @pl.when(me == 1)
    def _():
        first_to_sibling.wait_recv()
        first_all()

    for n in range(2):
        to_sibling(n).wait_recv()
        owner_core = lax.rem(dates_ref[n + 1] // DATE_DEV, 2)
        merged[n] = halves[n][owner_core]

        @pl.loop(1, CHIPS)
        def _(i):
            gather(n, other(i)).start()

        pieces[n][chip] = merged[n, chip]

    def part(n, k):
        return refs.at[n, core, k]

    def spread_out(n, k):
        return remote(part(n, chip), part(n, chip), spread_send.at[n, k], spread_recv.at[n, chip], same_core(k))

    def spread_in(n, k):
        return remote(part(n, k), part(n, k), spread_send.at[n, k], spread_recv.at[n, k], same_core(k))

    def inward(n, k):
        return remote(part(n, k), part(n, k), inward_send.at[n, k], inward_recv.at[n, k], sibling)

    def inward_in(n, k):
        there = refs.at[n, 1 - core, k]
        return remote(there, there, inward_send.at[n, k], inward_recv.at[n, k], sibling)

    def spread_all(n):
        @pl.loop(1, CHIPS)
        def _(i):
            spread_out(n, other(i)).start()

        inward(n, chip).start()

    @pl.when(chip > 0)
    def _():
        first_out(chip).wait_recv()

    spread_all(0)

    to_right.wait()
    to_left.wait()
    has_top = (tile > 0).astype(jnp.float32)
    has_bottom = (tile < tiles - 1).astype(jnp.float32)

    def first_edges_out(k, to):
        return remote(first_edges, first_edges, top_send.at[k], top_recv.at[0], to)

    @pl.when(me == 0)
    def _():
        first_edges[0:4] = left[0, 0:4]
        first_edges[4:8] = right[0, 0:4]

        @pl.loop(1, CHIPS)
        def _(k):
            first_edges_out(k, same_core(k)).start()

        first_edges_out(0, sibling).start()

    def take(n):
        @pl.loop(1, CHIPS)
        def _(i):
            gathered(n, other(i)).wait_recv()

        refs[n + 1, core, chip] = pieces[n][dates_ref[n + 1] // (2 * DATE_DEV)]

    take(0)
    spread_all(1)
    take(1)

    below = (core == 0) & (lax.rem(chip, 4) == 0)
    above = (core == 1) & (lax.rem(chip, 4) == 3)
    own_kind = jnp.where(core == 0, 0, 2) + chip // 4

    def rim_over(to):
        return remote(packed, ref_edges.at[own_kind], rim_send.at[0], rim_recv.at[4], to)

    @pl.when(below)
    def _():
        for s in range(REFS):
            packed[2 * s : 2 * s + 2] = refs[s, core, chip, 0:2]
        packed[6:8] = jnp.zeros((2, COLS), jnp.float32)
        rim_over(last_tile).start()

    @pl.when(above)
    def _():
        for s in range(REFS):
            packed[2 * s : 2 * s + 2] = refs[s, core, chip, 6:8]
        packed[6:8] = jnp.zeros((2, COLS), jnp.float32)
        rim_over(next_tile).start()

    spread_all(2)

    def rim_out(k):
        return remote(ref_edges.at[own_kind], ref_edges.at[own_kind], rim_send.at[1 + k], rim_recv.at[own_kind], same_core(k))

    def rim_in(kind):
        return remote(ref_edges.at[kind], ref_edges.at[kind], rim_send.at[0], rim_recv.at[kind], sibling)

    def rim_inward(kind):
        return remote(ref_edges.at[kind], ref_edges.at[kind], rim_in_send.at[kind], rim_in_recv.at[kind], sibling)

    def pass_on(n):
        @pl.loop(1, CHIPS)
        def _(i):
            k = other(i)
            spread_in(n, k).wait_recv()
            inward(n, k).start()

    def passed_on(n):
        @pl.loop(0, CHIPS)
        def _(k):
            inward_in(n, k).wait_recv()

    @pl.when(me > 0)
    def _():
        first_edges_out(0, sibling).wait_recv()

    @pl.when((me > 0) & (core == 0))
    def _():
        first_edges_out(0, sibling).start()

    @pl.when(below | above)
    def _():
        rim_over(next_tile).wait_recv()

        @pl.loop(1, CHIPS)
        def _(i):
            rim_out(other(i)).start()

        rim_inward(own_kind).start()

    pass_on(0)

    @pl.loop(0, DATE_DEV)
    def _(j):
        offset = offsets_ref[me * DATE_DEV + j]

        def shifted(x):
            for step in (1, 2, 4):
                x = jnp.where(lax.rem(offset // step, 2) == 1, pltpu.roll(x, COLS - step, 1), x)
            column = lax.broadcasted_iota(jnp.int32, x.shape, 1)
            return jnp.where(column < COLS - offset, x, 0.0)

        def edges_of(side):
            both = side[j // 2]
            return jnp.where(lax.rem(j, 2) == 0, both[0:4], both[4:8])

        above_rows = shifted(edges_of(left)) * has_top
        below_rows = shifted(edges_of(right)) * has_bottom
        lay(b_ext.at[j], 0, shifted(re_ref[j]), above_rows[0:2], below_rows[0:2])
        lay(b_ext.at[j], 1, shifted(im_ref[j]), above_rows[2:4], below_rows[2:4])
        power(b_ext.at[j], pow_b.at[j], prod, wide, band)

    passed_on(0)
    for p in range(2):
        rows = refs[0, :, 4 * p : 4 * p + 4].reshape(ROWS, COLS)
        top = first_edges[2 * p : 2 * p + 2] * has_top
        bottom = first_edges[2 * p + 4 : 2 * p + 6] * has_bottom
        lay(a_ext, p, rows, top, bottom)
    power(a_ext, pow_a, prod, wide, band)

    @pl.loop(0, DATE_DEV)
    def _(j):
        coherence(a_ext, pow_a, b_ext.at[j], pow_b.at[j], first_re.at[j], first_im.at[j], prod, wide, band)

    pass_on(1)

    @pl.loop(0, 2)
    def _(m):
        kind = core * 2 + m

        @pl.when(jnp.logical_not((below | above) & (kind == own_kind)))
        def _():
            rim_in(kind).wait_recv()
            rim_inward(kind).start()

    pass_on(2)
    passed_on(1)
    passed_on(2)

    @pl.loop(0, 2)
    def _(m):
        rim_inward((1 - core) * 2 + m).wait_recv()
        rim_inward(core * 2 + m).wait_send()

    to_sibling(0).wait_send()
    to_sibling(1).wait_send()

    @pl.when(core == 0)
    def _():
        first_edges_out(0, sibling).wait_send()

    @pl.when(me == 0)
    def _():
        first_to_sibling.wait_send()

        @pl.loop(1, CHIPS)
        def _(k):
            first_edges_out(k, same_core(k)).wait_send()

    @pl.when(chip == 0)
    def _():
        @pl.loop(1, CHIPS)
        def _(k):
            first_out(k).wait_send()

    @pl.when(below | above)
    def _():
        rim_over(next_tile).wait_send()

        @pl.loop(1, CHIPS)
        def _(i):
            rim_out(other(i)).wait_send()

    for n in range(2):

        @pl.loop(1, CHIPS)
        def _(i):
            gather(n, other(i)).wait_send()

    for n in range(REFS):

        @pl.loop(1, CHIPS)
        def _(i):
            spread_out(n, other(i)).wait_send()
            inward(n, other(i)).wait_send()

        inward(n, chip).wait_send()


def spread(dates, offsets, slc_re, slc_im):
    vmem = pl.BlockSpec(memory_space=pltpu.VMEM)
    hbm = pl.BlockSpec(memory_space=pltpu.HBM)
    dates_all = offsets.shape[0]
    f32 = jnp.float32
    dma = pltpu.SemaphoreType.DMA
    return pl.pallas_call(
        spread_kernel,
        out_shape=(
            jax.ShapeDtypeStruct((REFS, 2, CHIPS, 8, COLS), f32),
            jax.ShapeDtypeStruct((4, 8, COLS), f32),
            jax.ShapeDtypeStruct((2, 8, COLS), f32),
            jax.ShapeDtypeStruct((2, 8, COLS), f32),
            jax.ShapeDtypeStruct((DATE_DEV, 2, BLOCKS, 72, 128), f32),
            jax.ShapeDtypeStruct((DATE_DEV, BLOCKS, ROWS, 128), f32),
            jax.ShapeDtypeStruct((DATE_DEV, ROWS, COLS), f32),
            jax.ShapeDtypeStruct((DATE_DEV, ROWS, COLS), f32),
        ),
        in_specs=[hbm] * 4,
        out_specs=(vmem,) * 8,
        scratch_shapes=[
            pltpu.SMEM((STEPS,), jnp.int32),
            pltpu.SMEM((dates_all,), jnp.int32),
            pltpu.VMEM((DATE_DEV, ROWS, COLS), f32),
            pltpu.VMEM((DATE_DEV, ROWS, COLS), f32),
            pltpu.VMEM((256, 256), jnp.bfloat16),
            pltpu.VMEM((2, BLOCKS, 72, 128), f32),
            pltpu.VMEM((BLOCKS, 2 * ROWS, 256), jnp.bfloat16),
            pltpu.VMEM((2, BLOCKS, 72, 128), f32),
            pltpu.VMEM((BLOCKS, ROWS, 128), f32),
            dma((4,)),
            pltpu.VMEM((8, COLS), f32),
            pltpu.VMEM((2, 8, COLS), f32),
            pltpu.VMEM((2, 8, COLS), f32),
            pltpu.VMEM((8, COLS), f32),
            pltpu.VMEM((REFS, CHIPS, 8, COLS), f32),
            pltpu.VMEM((2, CHIPS, 8, COLS), f32),
            pltpu.VMEM((2, CHIPS, 8, COLS), f32),
            pltpu.VMEM((CHIPS, 8, COLS), f32),
            pltpu.VMEM((2, CHIPS, 8, COLS), f32),
            pltpu.VMEM((CHIPS, 8, COLS), f32),
            pltpu.VMEM((CHIPS, 8, COLS), f32),
            dma((3,)),
            dma((3,)),
            dma((2,)),
            dma((2,)),
            dma((CHIPS,)),
            dma((1,)),
            dma((2, CHIPS)),
            dma((2, CHIPS)),
            dma((REFS, CHIPS)),
            dma((REFS, CHIPS)),
            dma((REFS, CHIPS)),
            dma((REFS, CHIPS)),
            dma((CHIPS + 1,)),
            dma((5,)),
            dma((4,)),
            dma((4,)),
            dma((CHIPS,)),
            dma((1,)),
        ],
        compiler_params=pltpu.CompilerParams(collective_id=0, has_side_effects=True, vmem_limit_bytes=VMEM_LIMIT),
        name="spread",
    )(dates, offsets, slc_re, slc_im)


def compute_kernel(
    dates_hbm,
    keep_hbm,
    re_hbm,
    im_hbm,
    left,
    right,
    refs,
    ref_edges,
    b_ext,
    pow_b,
    first_re,
    first_im,
    out_re,
    out_im,
    dates_ref,
    keep_ref,
    band,
    own,
    zeros,
    stage,
    a_ext,
    prod,
    wide,
    pow_a,
    own_sems,
    out_sems,
):
    me = lax.axis_index("date")
    tile = lax.axis_index("tile")
    has_top = (tile > 0).astype(jnp.float32)
    has_bottom = (tile < lax.axis_size("tile") - 1).astype(jnp.float32)
    outs = (out_re, out_im)

    def zero_out(s, j, p):
        return pltpu.make_async_copy(zeros, outs[p].at[s, j], out_sems.at[p, s, j])

    def value_out(s, j, p):
        return pltpu.make_async_copy(stage.at[p, s - 1, j], outs[p].at[s, j], out_sems.at[p, s, j])

    def first_out(j, p):
        return pltpu.make_async_copy((first_re, first_im)[p].at[j], outs[p].at[0, j], out_sems.at[p, 0, j])

    slot = DATE_DEV - 2
    own_loads = [pltpu.make_async_copy(h.at[slot], own.at[p], own_sems.at[p]) for p, h in enumerate((re_hbm, im_hbm))]

    def valid(s, j):
        date = me * DATE_DEV + j
        return (keep_ref[s, date] == 1) & (date > dates_ref[s])

    scalars = ((dates_hbm, dates_ref), (keep_hbm, keep_ref))
    loads = [pltpu.make_async_copy(a, b, own_sems.at[2 + k]) for k, (a, b) in enumerate(scalars)]
    for c in loads:
        c.start()
    zeros[...] = jnp.zeros_like(zeros)
    band[...] = band_matrix()
    for c in loads:
        c.wait()

    @pl.loop(0, STEPS)
    def _(s):
        @pl.loop(0, DATE_DEV)
        def _(j):
            @pl.when(jnp.logical_not(valid(s, j)))
            def _():
                zero_out(s, j, 0).start()
                zero_out(s, j, 1).start()

    @pl.loop(0, DATE_DEV)
    def _(j):
        @pl.when(valid(0, j))
        def _():
            first_out(j, 0).start()
            first_out(j, 1).start()

    last = valid(REFS, DATE_DEV - 1)

    @pl.when(last)
    def _():
        for c in own_loads:
            c.start()

    def edge_rows(tile_rows, at):
        return jnp.where(at == 0, tile_rows[0:2], jnp.where(at == 1, tile_rows[2:4], tile_rows[4:6]))

    @pl.loop(1, STEPS)
    def _(s):
        some = valid(s, 0) | valid(s, 1) | valid(s, 2) | valid(s, 3)

        @pl.when(some & (s < REFS))
        def _():
            at = jnp.minimum(s, REFS - 1)
            for p in range(2):
                rows = refs[at, :, 4 * p : 4 * p + 4].reshape(ROWS, COLS)
                top = edge_rows(ref_edges[2 + p], at) * has_top
                bottom = edge_rows(ref_edges[p], at) * has_bottom
                lay(a_ext, p, rows, top, bottom)

        @pl.when(some & (s == REFS))
        def _():
            for c in own_loads:
                c.wait()
            for p in range(2):
                top = left[slot // 2, 2 * p : 2 * p + 2] * has_top
                bottom = right[slot // 2, 2 * p : 2 * p + 2] * has_bottom
                lay(a_ext, p, own[p], top, bottom)

        @pl.when(some)
        def _():
            power(a_ext, pow_a, prod, wide, band)

        @pl.loop(0, DATE_DEV)
        def _(j):
            @pl.when(valid(s, j))
            def _():
                coherence(a_ext, pow_a, b_ext.at[j], pow_b.at[j], stage.at[0, s - 1, j], stage.at[1, s - 1, j], prod, wide, band)
                value_out(s, j, 0).start()
                value_out(s, j, 1).start()

    @pl.loop(0, STEPS)
    def _(s):
        @pl.loop(0, DATE_DEV)
        def _(j):
            zero_out(s, j, 0).wait()
            zero_out(s, j, 1).wait()


def compute(dates, keep, slc_re, slc_im, *parts):
    vmem = pl.BlockSpec(memory_space=pltpu.VMEM)
    hbm = pl.BlockSpec(memory_space=pltpu.HBM)
    shape = jax.ShapeDtypeStruct((STEPS, DATE_DEV, ROWS, COLS), jnp.float32)
    f32 = jnp.float32
    return pl.pallas_call(
        compute_kernel,
        out_shape=(shape, shape),
        in_specs=[hbm] * 4 + [vmem] * len(parts),
        out_specs=(hbm, hbm),
        scratch_shapes=[
            pltpu.SMEM((STEPS,), jnp.int32),
            pltpu.SMEM(keep.shape, jnp.int32),
            pltpu.VMEM((256, 256), jnp.bfloat16),
            pltpu.VMEM((2, ROWS, COLS), f32),
            pltpu.VMEM((ROWS, COLS), f32),
            pltpu.VMEM((2, REFS, DATE_DEV, ROWS, COLS), f32),
            pltpu.VMEM((2, BLOCKS, 72, 128), f32),
            pltpu.VMEM((2, BLOCKS, 72, 128), f32),
            pltpu.VMEM((BLOCKS, 2 * ROWS, 256), jnp.bfloat16),
            pltpu.VMEM((BLOCKS, ROWS, 128), f32),
            pltpu.SemaphoreType.DMA((4,)),
            pltpu.SemaphoreType.DMA((2, STEPS, DATE_DEV)),
        ],
        compiler_params=pltpu.CompilerParams(vmem_limit_bytes=VMEM_LIMIT),
        name="coherence",
    )(dates, keep, slc_re, slc_im, *parts)


def body(slc_re, slc_im, ref_dates, pair_keep, col_offsets):
    hbm = [pltpu.with_memory_space_constraint(x, pltpu.HBM) for x in (slc_re, slc_im, ref_dates, pair_keep, col_offsets)]
    slc_re, slc_im, ref_dates, pair_keep, col_offsets = hbm
    parts = spread(ref_dates, col_offsets, slc_re, slc_im)
    order = (2, 3, 0, 1, 4, 5, 6, 7)
    return compute(ref_dates, pair_keep, slc_re, slc_im, *[parts[k] for k in order])


def solution(mesh):
    placed = (P("date", "tile", None), P("date", "tile", None), P(), P(), P())
    return jax.shard_map(
        body,
        mesh=mesh,
        in_specs=placed,
        out_specs=(P(None, "date", "tile", None), P(None, "date", "tile", None)),
        check_vma=False,
    )
```

```python
import jax
import jax.numpy as jnp
from jax import lax
from jax.experimental import pallas as pl
from jax.experimental.pallas import tpu as pltpu
from jax.sharding import PartitionSpec as P

MESH = pl.DeviceIdType.MESH
DATE_DEV = 4
ROWS = 64
COLS = 1024
BLOCKS = COLS // 128
REFS = 3
STEPS = 4
VMEM_LIMIT = 24 * 2**20


def band_matrix():
    k = lax.rem(lax.broadcasted_iota(jnp.int32, (256, 256), 0), 128)
    c = lax.broadcasted_iota(jnp.int32, (256, 256), 1)
    within = (c < 128) & (k >= c - 10) & (k <= c + 9)
    after = (c >= 128) & (c < 138) & (k >= c - 10)
    before = (c >= 247) & (k <= c - 247)
    return jnp.where(within | after | before, 1.0, 0.0).astype(jnp.bfloat16)


def lay(ext, plane, rows, top, bottom):
    for g in range(BLOCKS):
        cut = slice(128 * g, 128 * g + 128)
        ext[plane, g, 0:2] = top[:, cut]
        ext[plane, g, 2 : ROWS + 2] = rows[:, cut]
        ext[plane, g, ROWS + 2 : ROWS + 4] = bottom[:, cut]


def widen(prod, wide, count):
    for g in range(BLOCKS):
        for p in range(count):
            total = prod[p, g, 0:ROWS]
            for k in range(1, 5):
                total = total + prod[p, g, k : k + ROWS]
            high = total.astype(jnp.bfloat16)
            low = (total - high.astype(jnp.float32)).astype(jnp.bfloat16)
            wide[g, p * ROWS : (p + 1) * ROWS, 0:128] = high
            wide[g, p * ROWS : (p + 1) * ROWS, 128:256] = low


def columns(wide, band, count):
    rows = count * ROWS
    lhs = wide[:, 0:rows, :].reshape(BLOCKS * rows, 256)
    return jnp.dot(lhs, band[...], preferred_element_type=jnp.float32).reshape(BLOCKS, rows, 256)


def joined(sums, g, p):
    lane = lax.broadcasted_iota(jnp.int32, (ROWS, 128), 1)
    rows = slice(p * ROWS, (p + 1) * ROWS)
    zero = jnp.zeros((ROWS, 128), jnp.float32)
    before = sums[g - 1, rows, 128:256] if g > 0 else zero
    after = sums[g + 1, rows, 128:256] if g < BLOCKS - 1 else zero
    return sums[g, rows, 0:128] + jnp.where(lane < 64, before, after)


def power(ext, out, prod, wide, band):
    for g in range(BLOCKS):
        prod[0, g] = ext[0, g] * ext[0, g] + ext[1, g] * ext[1, g]
    widen(prod, wide, 1)
    sums = columns(wide, band, 1)
    for g in range(BLOCKS):
        out[g] = joined(sums, g, 0)


def coherence(a_ext, pow_a, b_ext, pow_b, out_re, out_im, prod, wide, band):
    for g in range(BLOCKS):
        a_re, a_im = a_ext[0, g], a_ext[1, g]
        b_re, b_im = b_ext[0, g], b_ext[1, g]
        prod[0, g] = a_re * b_re + a_im * b_im
        prod[1, g] = a_im * b_re - a_re * b_im
    widen(prod, wide, 2)
    sums = columns(wide, band, 2)
    for g in range(BLOCKS):
        scale = lax.rsqrt(pow_a[g] * pow_b[g] + 1e-06)
        for p, out in ((0, out_re), (1, out_im)):
            out[:, 128 * g : 128 * g + 128] = joined(sums, g, p) * scale


CHIPS = 8


def spread_kernel(
    dates_hbm,
    offsets_hbm,
    re_hbm,
    im_hbm,
    refs,
    ref_edges,
    left,
    right,
    b_ext,
    pow_b,
    first_re,
    first_im,
    dates_ref,
    offsets_ref,
    re_ref,
    im_ref,
    band,
    prod,
    wide,
    a_ext,
    pow_a,
    load_sems,
    first_edges,
    edges_right,
    edges_left,
    packed,
    outward,
    second_halves,
    third_halves,
    first_half,
    merged,
    second_pieces,
    third_pieces,
    pair_send,
    pair_recv,
    edge_send,
    edge_recv,
    first_send,
    first_recv,
    gather_send,
    gather_recv,
    spread_send,
    spread_recv,
    inward_send,
    inward_recv,
    rim_send,
    rim_recv,
    rim_in_send,
    rim_in_recv,
    top_send,
    top_recv,
):
    me = lax.axis_index("date")
    tile = lax.axis_index("tile")
    chip, core = me // 2, me % 2
    halves = (second_halves, third_halves)
    pieces = (second_pieces, third_pieces)
    tiles = lax.axis_size("tile")
    next_tile = {"tile": lax.rem(tile + 1, tiles)}
    last_tile = {"tile": lax.rem(tile + tiles - 1, tiles)}
    sibling = {"date": chip * 2 + 1 - core}

    def same_core(k):
        return {"date": k * 2 + core}

    def other(i):
        return lax.rem(chip + i, CHIPS)

    def remote(source, target, send, recv, to):
        return pltpu.make_async_remote_copy(src_ref=source, dst_ref=target, send_sem=send, recv_sem=recv, device_id=to, device_id_type=MESH)

    sources = ((dates_hbm, dates_ref), (offsets_hbm, offsets_ref), (re_hbm, re_ref), (im_hbm, im_ref))
    loads = [pltpu.make_async_copy(a, b, load_sems.at[k]) for k, (a, b) in enumerate(sources)]
    for c in loads:
        c.start()

    barrier = pltpu.get_barrier_semaphore()

    def greet(target):
        pl.semaphore_signal(barrier, inc=1, device_id=target, device_id_type=MESH)

    @pl.loop(1, CHIPS)
    def _(i):
        greet(same_core(other(i)))

    greet(next_tile)
    greet(last_tile)
    greet(sibling)
    band[...] = band_matrix()

    for c in loads:
        c.wait()

    def half(slot, c):
        rows = pl.ds(pl.multiple_of(c * 32, 32), 32)
        return re_ref[slot, rows].reshape(4, 8, COLS), im_ref[slot, rows].reshape(4, 8, COLS)

    for s in range(1, REFS):
        slot = lax.rem(dates_ref[s], DATE_DEV)
        halves[s - 1][core, 0:4], halves[s - 1][core, 4:8] = half(slot, core)
        outward[s - 1, 0:4], outward[s - 1, 4:8] = half(slot, 1 - core)

    @pl.when(me == 0)
    def _():
        first_half[0:4], first_half[4:8] = half(0, 0)
        outward[REFS - 1, 0:4], outward[REFS - 1, 4:8] = half(0, 1)

    for j in range(DATE_DEV):
        at = 4 * (j % 2)
        for p, plane in enumerate((re_ref, im_ref)):
            edges_right[j // 2, at + 2 * p : at + 2 * p + 2] = plane[j, ROWS - 2 : ROWS]
            edges_left[j // 2, at + 2 * p : at + 2 * p + 2] = plane[j, 0:2]

    pl.semaphore_wait(barrier, 10)

    def to_sibling(n):
        return remote(outward.at[n], halves[n].at[core], pair_send.at[n], pair_recv.at[n], sibling)

    first_to_sibling = remote(outward.at[REFS - 1], first_half, pair_send.at[2], pair_recv.at[2], sibling)
    to_sibling(0).start()
    to_right = remote(edges_right, left, edge_send.at[0], edge_recv.at[0], next_tile)
    to_left = remote(edges_left, right, edge_send.at[1], edge_recv.at[1], last_tile)
    to_right.start()
    to_left.start()

    def first_out(k):
        return remote(first_half.at[k], refs.at[0, core, k], first_send.at[k], first_recv.at[0], same_core(k))

    def first_all():
        refs[0, core, 0] = first_half[0]

        @pl.loop(1, CHIPS)
        def _(k):
            first_out(k).start()

    @pl.when(me == 0)
    def _():
        first_to_sibling.start()
        first_all()

    to_sibling(1).start()

    def gather(n, k):
        return remote(merged.at[n, k], pieces[n].at[chip], gather_send.at[n, k], gather_recv.at[n, chip], same_core(k))

    def gathered(n, k):
        return remote(merged.at[n, k], pieces[n].at[k], gather_send.at[n, k], gather_recv.at[n, k], same_core(k))

    @pl.when(me == 1)
    def _():
        first_to_sibling.wait_recv()
        first_all()

    for n in range(2):
        to_sibling(n).wait_recv()
        owner_core = lax.rem(dates_ref[n + 1] // DATE_DEV, 2)
        merged[n] = halves[n][owner_core]

        @pl.loop(1, CHIPS)
        def _(i):
            gather(n, other(i)).start()

        pieces[n][chip] = merged[n, chip]

    def part(n, k):
        return refs.at[n, core, k]

    def spread_out(n, k):
        return remote(part(n, chip), part(n, chip), spread_send.at[n, k], spread_recv.at[n, chip], same_core(k))

    def spread_in(n, k):
        return remote(part(n, k), part(n, k), spread_send.at[n, k], spread_recv.at[n, k], same_core(k))

    def inward(n, k):
        return remote(part(n, k), part(n, k), inward_send.at[n, k], inward_recv.at[n, k], sibling)

    def inward_in(n, k):
        there = refs.at[n, 1 - core, k]
        return remote(there, there, inward_send.at[n, k], inward_recv.at[n, k], sibling)

    def spread_all(n):
        @pl.loop(1, CHIPS)
        def _(i):
            spread_out(n, other(i)).start()

        inward(n, chip).start()

    @pl.when(chip > 0)
    def _():
        first_out(chip).wait_recv()

    spread_all(0)

    to_right.wait()
    to_left.wait()
    has_top = (tile > 0).astype(jnp.float32)
    has_bottom = (tile < tiles - 1).astype(jnp.float32)

    def first_edges_out(k, to):
        return remote(first_edges, first_edges, top_send.at[k], top_recv.at[0], to)

    @pl.when(me == 0)
    def _():
        first_edges[0:4] = left[0, 0:4]
        first_edges[4:8] = right[0, 0:4]

        @pl.loop(1, CHIPS)
        def _(k):
            first_edges_out(k, same_core(k)).start()

        first_edges_out(0, sibling).start()

    def take(n):
        @pl.loop(1, CHIPS)
        def _(i):
            gathered(n, other(i)).wait_recv()

        refs[n + 1, core, chip] = pieces[n][dates_ref[n + 1] // (2 * DATE_DEV)]

    take(0)
    spread_all(1)
    take(1)

    below = (core == 0) & (lax.rem(chip, 4) == 0)
    above = (core == 1) & (lax.rem(chip, 4) == 3)
    own_kind = jnp.where(core == 0, 0, 2) + chip // 4

    def rim_over(to):
        return remote(packed, ref_edges.at[own_kind], rim_send.at[0], rim_recv.at[4], to)

    @pl.when(below)
    def _():
        for s in range(REFS):
            packed[2 * s : 2 * s + 2] = refs[s, core, chip, 0:2]
        packed[6:8] = jnp.zeros((2, COLS), jnp.float32)
        rim_over(last_tile).start()

    @pl.when(above)
    def _():
        for s in range(REFS):
            packed[2 * s : 2 * s + 2] = refs[s, core, chip, 6:8]
        packed[6:8] = jnp.zeros((2, COLS), jnp.float32)
        rim_over(next_tile).start()

    def rim_out(k):
        return remote(ref_edges.at[own_kind], ref_edges.at[own_kind], rim_send.at[1 + k], rim_recv.at[own_kind], same_core(k))

    def rim_in(kind):
        return remote(ref_edges.at[kind], ref_edges.at[kind], rim_send.at[0], rim_recv.at[kind], sibling)

    def rim_inward(kind):
        return remote(ref_edges.at[kind], ref_edges.at[kind], rim_in_send.at[kind], rim_in_recv.at[kind], sibling)

    @pl.when(below | above)
    def _():
        rim_over(next_tile).wait_recv()

        @pl.loop(1, CHIPS)
        def _(i):
            rim_out(other(i)).start()

        rim_inward(own_kind).start()

    spread_all(2)

    def pass_on(n):
        @pl.loop(1, CHIPS)
        def _(i):
            k = other(i)
            spread_in(n, k).wait_recv()
            inward(n, k).start()

    def passed_on(n):
        @pl.loop(0, CHIPS)
        def _(k):
            inward_in(n, k).wait_recv()

    @pl.when(me > 0)
    def _():
        first_edges_out(0, sibling).wait_recv()

    @pl.when((me > 0) & (core == 0))
    def _():
        first_edges_out(0, sibling).start()

    pass_on(0)

    @pl.loop(0, DATE_DEV)
    def _(j):
        offset = offsets_ref[me * DATE_DEV + j]

        def shifted(x):
            for step in (1, 2, 4):
                x = jnp.where(lax.rem(offset // step, 2) == 1, pltpu.roll(x, COLS - step, 1), x)
            column = lax.broadcasted_iota(jnp.int32, x.shape, 1)
            return jnp.where(column < COLS - offset, x, 0.0)

        def edges_of(side):
            both = side[j // 2]
            return jnp.where(lax.rem(j, 2) == 0, both[0:4], both[4:8])

        above_rows = shifted(edges_of(left)) * has_top
        below_rows = shifted(edges_of(right)) * has_bottom
        lay(b_ext.at[j], 0, shifted(re_ref[j]), above_rows[0:2], below_rows[0:2])
        lay(b_ext.at[j], 1, shifted(im_ref[j]), above_rows[2:4], below_rows[2:4])
        power(b_ext.at[j], pow_b.at[j], prod, wide, band)

    passed_on(0)
    for p in range(2):
        rows = refs[0, :, 4 * p : 4 * p + 4].reshape(ROWS, COLS)
        top = first_edges[2 * p : 2 * p + 2] * has_top
        bottom = first_edges[2 * p + 4 : 2 * p + 6] * has_bottom
        lay(a_ext, p, rows, top, bottom)
    power(a_ext, pow_a, prod, wide, band)

    @pl.loop(0, DATE_DEV)
    def _(j):
        coherence(a_ext, pow_a, b_ext.at[j], pow_b.at[j], first_re.at[j], first_im.at[j], prod, wide, band)

    pass_on(1)

    @pl.loop(0, 2)
    def _(m):
        kind = core * 2 + m

        @pl.when(jnp.logical_not((below | above) & (kind == own_kind)))
        def _():
            rim_in(kind).wait_recv()
            rim_inward(kind).start()

    pass_on(2)
    passed_on(1)
    passed_on(2)

    @pl.loop(0, 2)
    def _(m):
        rim_inward((1 - core) * 2 + m).wait_recv()
        rim_inward(core * 2 + m).wait_send()

    to_sibling(0).wait_send()
    to_sibling(1).wait_send()

    @pl.when(core == 0)
    def _():
        first_edges_out(0, sibling).wait_send()

    @pl.when(me == 0)
    def _():
        first_to_sibling.wait_send()

        @pl.loop(1, CHIPS)
        def _(k):
            first_edges_out(k, same_core(k)).wait_send()

    @pl.when(chip == 0)
    def _():
        @pl.loop(1, CHIPS)
        def _(k):
            first_out(k).wait_send()

    @pl.when(below | above)
    def _():
        rim_over(next_tile).wait_send()

        @pl.loop(1, CHIPS)
        def _(i):
            rim_out(other(i)).wait_send()

    for n in range(2):

        @pl.loop(1, CHIPS)
        def _(i):
            gather(n, other(i)).wait_send()

    for n in range(REFS):

        @pl.loop(1, CHIPS)
        def _(i):
            spread_out(n, other(i)).wait_send()
            inward(n, other(i)).wait_send()

        inward(n, chip).wait_send()


def spread(dates, offsets, slc_re, slc_im):
    vmem = pl.BlockSpec(memory_space=pltpu.VMEM)
    hbm = pl.BlockSpec(memory_space=pltpu.HBM)
    dates_all = offsets.shape[0]
    f32 = jnp.float32
    dma = pltpu.SemaphoreType.DMA
    return pl.pallas_call(
        spread_kernel,
        out_shape=(
            jax.ShapeDtypeStruct((REFS, 2, CHIPS, 8, COLS), f32),
            jax.ShapeDtypeStruct((4, 8, COLS), f32),
            jax.ShapeDtypeStruct((2, 8, COLS), f32),
            jax.ShapeDtypeStruct((2, 8, COLS), f32),
            jax.ShapeDtypeStruct((DATE_DEV, 2, BLOCKS, 72, 128), f32),
            jax.ShapeDtypeStruct((DATE_DEV, BLOCKS, ROWS, 128), f32),
            jax.ShapeDtypeStruct((DATE_DEV, ROWS, COLS), f32),
            jax.ShapeDtypeStruct((DATE_DEV, ROWS, COLS), f32),
        ),
        in_specs=[hbm] * 4,
        out_specs=(vmem,) * 8,
        scratch_shapes=[
            pltpu.SMEM((STEPS,), jnp.int32),
            pltpu.SMEM((dates_all,), jnp.int32),
            pltpu.VMEM((DATE_DEV, ROWS, COLS), f32),
            pltpu.VMEM((DATE_DEV, ROWS, COLS), f32),
            pltpu.VMEM((256, 256), jnp.bfloat16),
            pltpu.VMEM((2, BLOCKS, 72, 128), f32),
            pltpu.VMEM((BLOCKS, 2 * ROWS, 256), jnp.bfloat16),
            pltpu.VMEM((2, BLOCKS, 72, 128), f32),
            pltpu.VMEM((BLOCKS, ROWS, 128), f32),
            dma((4,)),
            pltpu.VMEM((8, COLS), f32),
            pltpu.VMEM((2, 8, COLS), f32),
            pltpu.VMEM((2, 8, COLS), f32),
            pltpu.VMEM((8, COLS), f32),
            pltpu.VMEM((REFS, CHIPS, 8, COLS), f32),
            pltpu.VMEM((2, CHIPS, 8, COLS), f32),
            pltpu.VMEM((2, CHIPS, 8, COLS), f32),
            pltpu.VMEM((CHIPS, 8, COLS), f32),
            pltpu.VMEM((2, CHIPS, 8, COLS), f32),
            pltpu.VMEM((CHIPS, 8, COLS), f32),
            pltpu.VMEM((CHIPS, 8, COLS), f32),
            dma((3,)),
            dma((3,)),
            dma((2,)),
            dma((2,)),
            dma((CHIPS,)),
            dma((1,)),
            dma((2, CHIPS)),
            dma((2, CHIPS)),
            dma((REFS, CHIPS)),
            dma((REFS, CHIPS)),
            dma((REFS, CHIPS)),
            dma((REFS, CHIPS)),
            dma((CHIPS + 1,)),
            dma((5,)),
            dma((4,)),
            dma((4,)),
            dma((CHIPS,)),
            dma((1,)),
        ],
        compiler_params=pltpu.CompilerParams(collective_id=0, has_side_effects=True, vmem_limit_bytes=VMEM_LIMIT),
        name="spread",
    )(dates, offsets, slc_re, slc_im)


def compute_kernel(
    dates_hbm,
    keep_hbm,
    re_hbm,
    im_hbm,
    left,
    right,
    refs,
    ref_edges,
    b_ext,
    pow_b,
    first_re,
    first_im,
    out_re,
    out_im,
    dates_ref,
    keep_ref,
    band,
    own,
    zeros,
    stage,
    a_ext,
    prod,
    wide,
    pow_a,
    own_sems,
    out_sems,
):
    me = lax.axis_index("date")
    tile = lax.axis_index("tile")
    has_top = (tile > 0).astype(jnp.float32)
    has_bottom = (tile < lax.axis_size("tile") - 1).astype(jnp.float32)
    outs = (out_re, out_im)

    def zero_out(s, j, p):
        return pltpu.make_async_copy(zeros, outs[p].at[s, j], out_sems.at[p, s, j])

    def value_out(s, j, p):
        return pltpu.make_async_copy(stage.at[p, s - 1, j], outs[p].at[s, j], out_sems.at[p, s, j])

    def first_out(j, p):
        return pltpu.make_async_copy((first_re, first_im)[p].at[j], outs[p].at[0, j], out_sems.at[p, 0, j])

    slot = DATE_DEV - 2
    own_loads = [pltpu.make_async_copy(h.at[slot], own.at[p], own_sems.at[p]) for p, h in enumerate((re_hbm, im_hbm))]

    def past_last(j):
        return me * DATE_DEV + j == lax.axis_size("date") * DATE_DEV - 1

    def valid(s, j):
        date = me * DATE_DEV + j
        return (keep_ref[s, date] == 1) & (date > dates_ref[s]) & ((s < REFS) | past_last(j))

    scalars = ((dates_hbm, dates_ref), (keep_hbm, keep_ref))
    loads = [pltpu.make_async_copy(a, b, own_sems.at[2 + k]) for k, (a, b) in enumerate(scalars)]
    for c in loads:
        c.start()
    zeros[...] = jnp.zeros_like(zeros)

    @pl.loop(0, DATE_DEV)
    def _(j):
        @pl.when(jnp.logical_not(past_last(j)))
        def _():
            zero_out(REFS, j, 0).start()
            zero_out(REFS, j, 1).start()

    band[...] = band_matrix()
    for c in loads:
        c.wait()

    @pl.loop(0, STEPS)
    def _(s):
        @pl.loop(0, DATE_DEV)
        def _(j):
            @pl.when(jnp.logical_not(valid(s, j)) & ((s < REFS) | past_last(j)))
            def _():
                zero_out(s, j, 0).start()
                zero_out(s, j, 1).start()

    @pl.loop(0, DATE_DEV)
    def _(j):
        @pl.when(valid(0, j))
        def _():
            first_out(j, 0).start()
            first_out(j, 1).start()

    last = valid(REFS, DATE_DEV - 1)

    @pl.when(last)
    def _():
        for c in own_loads:
            c.start()

    def edge_rows(tile_rows, at):
        return jnp.where(at == 0, tile_rows[0:2], jnp.where(at == 1, tile_rows[2:4], tile_rows[4:6]))

    @pl.loop(1, STEPS)
    def _(s):
        some = valid(s, 0) | valid(s, 1) | valid(s, 2) | valid(s, 3)

        @pl.when(some & (s < REFS))
        def _():
            at = jnp.minimum(s, REFS - 1)
            for p in range(2):
                rows = refs[at, :, 4 * p : 4 * p + 4].reshape(ROWS, COLS)
                top = edge_rows(ref_edges[2 + p], at) * has_top
                bottom = edge_rows(ref_edges[p], at) * has_bottom
                lay(a_ext, p, rows, top, bottom)

        @pl.when(some & (s == REFS))
        def _():
            for c in own_loads:
                c.wait()
            for p in range(2):
                top = left[slot // 2, 2 * p : 2 * p + 2] * has_top
                bottom = right[slot // 2, 2 * p : 2 * p + 2] * has_bottom
                lay(a_ext, p, own[p], top, bottom)

        @pl.when(some)
        def _():
            power(a_ext, pow_a, prod, wide, band)

        @pl.loop(0, DATE_DEV)
        def _(j):
            @pl.when(valid(s, j))
            def _():
                coherence(a_ext, pow_a, b_ext.at[j], pow_b.at[j], stage.at[0, s - 1, j], stage.at[1, s - 1, j], prod, wide, band)
                value_out(s, j, 0).start()
                value_out(s, j, 1).start()

    @pl.loop(0, STEPS)
    def _(s):
        @pl.loop(0, DATE_DEV)
        def _(j):
            zero_out(s, j, 0).wait()
            zero_out(s, j, 1).wait()


def compute(dates, keep, slc_re, slc_im, *parts):
    vmem = pl.BlockSpec(memory_space=pltpu.VMEM)
    hbm = pl.BlockSpec(memory_space=pltpu.HBM)
    shape = jax.ShapeDtypeStruct((STEPS, DATE_DEV, ROWS, COLS), jnp.float32)
    f32 = jnp.float32
    return pl.pallas_call(
        compute_kernel,
        out_shape=(shape, shape),
        in_specs=[hbm] * 4 + [vmem] * len(parts),
        out_specs=(hbm, hbm),
        scratch_shapes=[
            pltpu.SMEM((STEPS,), jnp.int32),
            pltpu.SMEM(keep.shape, jnp.int32),
            pltpu.VMEM((256, 256), jnp.bfloat16),
            pltpu.VMEM((2, ROWS, COLS), f32),
            pltpu.VMEM((ROWS, COLS), f32),
            pltpu.VMEM((2, REFS, DATE_DEV, ROWS, COLS), f32),
            pltpu.VMEM((2, BLOCKS, 72, 128), f32),
            pltpu.VMEM((2, BLOCKS, 72, 128), f32),
            pltpu.VMEM((BLOCKS, 2 * ROWS, 256), jnp.bfloat16),
            pltpu.VMEM((BLOCKS, ROWS, 128), f32),
            pltpu.SemaphoreType.DMA((4,)),
            pltpu.SemaphoreType.DMA((2, STEPS, DATE_DEV)),
        ],
        compiler_params=pltpu.CompilerParams(vmem_limit_bytes=VMEM_LIMIT),
        name="coherence",
    )(dates, keep, slc_re, slc_im, *parts)


def body(slc_re, slc_im, ref_dates, pair_keep, col_offsets):
    hbm = [pltpu.with_memory_space_constraint(x, pltpu.HBM) for x in (slc_re, slc_im, ref_dates, pair_keep, col_offsets)]
    slc_re, slc_im, ref_dates, pair_keep, col_offsets = hbm
    parts = spread(ref_dates, col_offsets, slc_re, slc_im)
    order = (2, 3, 0, 1, 4, 5, 6, 7)
    return compute(ref_dates, pair_keep, slc_re, slc_im, *[parts[k] for k in order])


def solution(mesh):
    placed = (P("date", "tile", None), P("date", "tile", None), P(), P(), P())
    return jax.shard_map(
        body,
        mesh=mesh,
        in_specs=placed,
        out_specs=(P(None, "date", "tile", None), P(None, "date", "tile", None)),
        check_vma=False,
    )
```

```python
import jax
import jax.numpy as jnp
from jax import lax
from jax.experimental import pallas as pl
from jax.experimental.pallas import tpu as pltpu
from jax.sharding import PartitionSpec as P

MESH = pl.DeviceIdType.MESH
DATE_DEV = 4
ROWS = 64
COLS = 1024
BLOCKS = COLS // 128
REFS = 3
STEPS = 4
VMEM_LIMIT = 24 * 2**20


def band_matrix():
    k = lax.rem(lax.broadcasted_iota(jnp.int32, (256, 256), 0), 128)
    c = lax.broadcasted_iota(jnp.int32, (256, 256), 1)
    within = (c < 128) & (k >= c - 10) & (k <= c + 9)
    after = (c >= 128) & (c < 138) & (k >= c - 10)
    before = (c >= 247) & (k <= c - 247)
    return jnp.where(within | after | before, 1.0, 0.0).astype(jnp.bfloat16)


def lay(ext, plane, rows, top, bottom):
    for g in range(BLOCKS):
        cut = slice(128 * g, 128 * g + 128)
        ext[plane, g, 0:2] = top[:, cut]
        ext[plane, g, 2 : ROWS + 2] = rows[:, cut]
        ext[plane, g, ROWS + 2 : ROWS + 4] = bottom[:, cut]


def widen(prod, wide, count):
    for g in range(BLOCKS):
        for p in range(count):
            total = prod[p, g, 0:ROWS]
            for k in range(1, 5):
                total = total + prod[p, g, k : k + ROWS]
            high = total.astype(jnp.bfloat16)
            low = (total - high.astype(jnp.float32)).astype(jnp.bfloat16)
            wide[g, p * ROWS : (p + 1) * ROWS, 0:128] = high
            wide[g, p * ROWS : (p + 1) * ROWS, 128:256] = low


def columns(wide, band, count):
    rows = count * ROWS
    lhs = wide[:, 0:rows, :].reshape(BLOCKS * rows, 256)
    return jnp.dot(lhs, band[...], preferred_element_type=jnp.float32).reshape(BLOCKS, rows, 256)


def joined(sums, g, p):
    lane = lax.broadcasted_iota(jnp.int32, (ROWS, 128), 1)
    rows = slice(p * ROWS, (p + 1) * ROWS)
    zero = jnp.zeros((ROWS, 128), jnp.float32)
    before = sums[g - 1, rows, 128:256] if g > 0 else zero
    after = sums[g + 1, rows, 128:256] if g < BLOCKS - 1 else zero
    return sums[g, rows, 0:128] + jnp.where(lane < 64, before, after)


def power(ext, out, prod, wide, band):
    for g in range(BLOCKS):
        prod[0, g] = ext[0, g] * ext[0, g] + ext[1, g] * ext[1, g]
    widen(prod, wide, 1)
    sums = columns(wide, band, 1)
    for g in range(BLOCKS):
        out[g] = joined(sums, g, 0)


def coherence(a_ext, pow_a, b_ext, pow_b, out_re, out_im, prod, wide, band):
    for g in range(BLOCKS):
        a_re, a_im = a_ext[0, g], a_ext[1, g]
        b_re, b_im = b_ext[0, g], b_ext[1, g]
        prod[0, g] = a_re * b_re + a_im * b_im
        prod[1, g] = a_im * b_re - a_re * b_im
    widen(prod, wide, 2)
    sums = columns(wide, band, 2)
    for g in range(BLOCKS):
        scale = lax.rsqrt(pow_a[g] * pow_b[g] + 1e-06)
        for p, out in ((0, out_re), (1, out_im)):
            out[:, 128 * g : 128 * g + 128] = joined(sums, g, p) * scale


CHIPS = 8


def spread_kernel(
    dates_hbm,
    offsets_hbm,
    re_hbm,
    im_hbm,
    refs,
    ref_edges,
    left,
    right,
    b_ext,
    pow_b,
    first_re,
    first_im,
    dates_ref,
    offsets_ref,
    re_ref,
    im_ref,
    band,
    prod,
    wide,
    a_ext,
    pow_a,
    load_sems,
    first_edges,
    edges_right,
    edges_left,
    packed,
    outward,
    second_halves,
    third_halves,
    first_half,
    merged,
    second_pieces,
    third_pieces,
    pair_send,
    pair_recv,
    edge_send,
    edge_recv,
    first_send,
    first_recv,
    gather_send,
    gather_recv,
    spread_send,
    spread_recv,
    inward_send,
    inward_recv,
    rim_send,
    rim_recv,
    rim_in_send,
    rim_in_recv,
    top_send,
    top_recv,
):
    me = lax.axis_index("date")
    tile = lax.axis_index("tile")
    chip, core = me // 2, me % 2
    halves = (second_halves, third_halves)
    pieces = (second_pieces, third_pieces)
    tiles = lax.axis_size("tile")
    next_tile = {"tile": lax.rem(tile + 1, tiles)}
    last_tile = {"tile": lax.rem(tile + tiles - 1, tiles)}
    sibling = {"date": chip * 2 + 1 - core}

    def same_core(k):
        return {"date": k * 2 + core}

    def other(i):
        return lax.rem(chip + i, CHIPS)

    def remote(source, target, send, recv, to):
        return pltpu.make_async_remote_copy(src_ref=source, dst_ref=target, send_sem=send, recv_sem=recv, device_id=to, device_id_type=MESH)

    sources = ((dates_hbm, dates_ref), (offsets_hbm, offsets_ref), (re_hbm, re_ref), (im_hbm, im_ref))
    loads = [pltpu.make_async_copy(a, b, load_sems.at[k]) for k, (a, b) in enumerate(sources)]
    for c in loads:
        c.start()

    barrier = pltpu.get_barrier_semaphore()

    def greet(target):
        pl.semaphore_signal(barrier, inc=1, device_id=target, device_id_type=MESH)

    @pl.loop(1, CHIPS)
    def _(i):
        greet(same_core(other(i)))

    greet(next_tile)
    greet(last_tile)
    greet(sibling)
    band[...] = band_matrix()

    for c in loads:
        c.wait()

    def half(slot, c):
        rows = pl.ds(pl.multiple_of(c * 32, 32), 32)
        return re_ref[slot, rows].reshape(4, 8, COLS), im_ref[slot, rows].reshape(4, 8, COLS)

    for s in range(1, REFS):
        slot = lax.rem(dates_ref[s], DATE_DEV)
        halves[s - 1][core, 0:4], halves[s - 1][core, 4:8] = half(slot, core)
        outward[s - 1, 0:4], outward[s - 1, 4:8] = half(slot, 1 - core)

    @pl.when(me == 0)
    def _():
        first_half[0:4], first_half[4:8] = half(0, 0)
        outward[REFS - 1, 0:4], outward[REFS - 1, 4:8] = half(0, 1)

    for j in range(DATE_DEV):
        at = 4 * (j % 2)
        for p, plane in enumerate((re_ref, im_ref)):
            edges_right[j // 2, at + 2 * p : at + 2 * p + 2] = plane[j, ROWS - 2 : ROWS]
            edges_left[j // 2, at + 2 * p : at + 2 * p + 2] = plane[j, 0:2]

    pl.semaphore_wait(barrier, 10)

    def to_sibling(n):
        return remote(outward.at[n], halves[n].at[core], pair_send.at[n], pair_recv.at[n], sibling)

    first_to_sibling = remote(outward.at[REFS - 1], first_half, pair_send.at[2], pair_recv.at[2], sibling)
    to_sibling(0).start()
    to_right = remote(edges_right, left, edge_send.at[0], edge_recv.at[0], next_tile)
    to_left = remote(edges_left, right, edge_send.at[1], edge_recv.at[1], last_tile)
    to_right.start()
    to_left.start()

    def first_out(k):
        return remote(first_half.at[k], refs.at[0, core, k], first_send.at[k], first_recv.at[0], same_core(k))

    def first_all():
        refs[0, core, 0] = first_half[0]

        @pl.loop(1, CHIPS)
        def _(k):
            first_out(k).start()

    @pl.when(me == 0)
    def _():
        first_to_sibling.start()
        first_all()

    to_sibling(1).start()

    def gather(n, k):
        return remote(merged.at[n, k], pieces[n].at[chip], gather_send.at[n, k], gather_recv.at[n, chip], same_core(k))

    def gathered(n, k):
        return remote(merged.at[n, k], pieces[n].at[k], gather_send.at[n, k], gather_recv.at[n, k], same_core(k))

    @pl.when(me == 1)
    def _():
        first_to_sibling.wait_recv()
        first_all()

    for n in range(2):
        to_sibling(n).wait_recv()
        owner_core = lax.rem(dates_ref[n + 1] // DATE_DEV, 2)
        merged[n] = halves[n][owner_core]

        @pl.loop(1, CHIPS)
        def _(i):
            gather(n, other(i)).start()

        pieces[n][chip] = merged[n, chip]

    def part(n, k):
        return refs.at[n, core, k]

    def spread_out(n, k):
        return remote(part(n, chip), part(n, chip), spread_send.at[n, k], spread_recv.at[n, chip], same_core(k))

    def spread_in(n, k):
        return remote(part(n, k), part(n, k), spread_send.at[n, k], spread_recv.at[n, k], same_core(k))

    def inward(n, k):
        return remote(part(n, k), part(n, k), inward_send.at[n, k], inward_recv.at[n, k], sibling)

    def inward_in(n, k):
        there = refs.at[n, 1 - core, k]
        return remote(there, there, inward_send.at[n, k], inward_recv.at[n, k], sibling)

    def spread_all(n):
        @pl.loop(1, CHIPS)
        def _(i):
            spread_out(n, other(i)).start()

        inward(n, chip).start()

    @pl.when(chip > 0)
    def _():
        first_out(chip).wait_recv()

    spread_all(0)

    to_right.wait()
    to_left.wait()
    has_top = (tile > 0).astype(jnp.float32)
    has_bottom = (tile < tiles - 1).astype(jnp.float32)

    def first_edges_out(k, to):
        return remote(first_edges, first_edges, top_send.at[k], top_recv.at[0], to)

    @pl.when(me == 0)
    def _():
        first_edges[0:4] = left[0, 0:4]
        first_edges[4:8] = right[0, 0:4]

        @pl.loop(1, CHIPS)
        def _(k):
            first_edges_out(k, same_core(k)).start()

        first_edges_out(0, sibling).start()

    def take(n):
        @pl.loop(1, CHIPS)
        def _(i):
            gathered(n, other(i)).wait_recv()

        refs[n + 1, core, chip] = pieces[n][dates_ref[n + 1] // (2 * DATE_DEV)]

    take(0)
    spread_all(1)
    take(1)

    below = (core == 0) & (lax.rem(chip, 4) == 0)
    above = (core == 1) & (lax.rem(chip, 4) == 3)
    own_kind = jnp.where(core == 0, 0, 2) + chip // 4

    def rim_over(to):
        return remote(packed, ref_edges.at[own_kind], rim_send.at[0], rim_recv.at[4], to)

    @pl.when(below)
    def _():
        for s in range(REFS):
            packed[2 * s : 2 * s + 2] = refs[s, core, chip, 0:2]
        packed[6:8] = jnp.zeros((2, COLS), jnp.float32)
        rim_over(last_tile).start()

    @pl.when(above)
    def _():
        for s in range(REFS):
            packed[2 * s : 2 * s + 2] = refs[s, core, chip, 6:8]
        packed[6:8] = jnp.zeros((2, COLS), jnp.float32)
        rim_over(next_tile).start()

    def rim_out(k):
        return remote(ref_edges.at[own_kind], ref_edges.at[own_kind], rim_send.at[1 + k], rim_recv.at[own_kind], same_core(k))

    def rim_in(kind):
        return remote(ref_edges.at[kind], ref_edges.at[kind], rim_send.at[0], rim_recv.at[kind], sibling)

    def rim_inward(kind):
        return remote(ref_edges.at[kind], ref_edges.at[kind], rim_in_send.at[kind], rim_in_recv.at[kind], sibling)

    @pl.when(below | above)
    def _():
        rim_over(next_tile).wait_recv()

        @pl.loop(1, CHIPS)
        def _(i):
            rim_out(other(i)).start()

        rim_inward(own_kind).start()

    spread_all(2)

    def pass_on(n):
        @pl.loop(1, CHIPS)
        def _(i):
            k = other(i)
            spread_in(n, k).wait_recv()
            inward(n, k).start()

    def passed_on(n):
        @pl.loop(0, CHIPS)
        def _(k):
            inward_in(n, k).wait_recv()

    @pl.when(me > 0)
    def _():
        first_edges_out(0, sibling).wait_recv()

    @pl.when((me > 0) & (core == 0))
    def _():
        first_edges_out(0, sibling).start()

    pass_on(0)

    @pl.loop(0, DATE_DEV)
    def _(j):
        offset = offsets_ref[me * DATE_DEV + j]

        def shifted(x):
            for step in (1, 2, 4):
                x = jnp.where(lax.rem(offset // step, 2) == 1, pltpu.roll(x, COLS - step, 1), x)
            column = lax.broadcasted_iota(jnp.int32, x.shape, 1)
            return jnp.where(column < COLS - offset, x, 0.0)

        def edges_of(side):
            both = side[j // 2]
            return jnp.where(lax.rem(j, 2) == 0, both[0:4], both[4:8])

        above_rows = shifted(edges_of(left)) * has_top
        below_rows = shifted(edges_of(right)) * has_bottom
        lay(b_ext.at[j], 0, shifted(re_ref[j]), above_rows[0:2], below_rows[0:2])
        lay(b_ext.at[j], 1, shifted(im_ref[j]), above_rows[2:4], below_rows[2:4])
        power(b_ext.at[j], pow_b.at[j], prod, wide, band)

    passed_on(0)
    for p in range(2):
        rows = refs[0, :, 4 * p : 4 * p + 4].reshape(ROWS, COLS)
        top = first_edges[2 * p : 2 * p + 2] * has_top
        bottom = first_edges[2 * p + 4 : 2 * p + 6] * has_bottom
        lay(a_ext, p, rows, top, bottom)
    power(a_ext, pow_a, prod, wide, band)

    @pl.loop(0, DATE_DEV)
    def _(j):
        coherence(a_ext, pow_a, b_ext.at[j], pow_b.at[j], first_re.at[j], first_im.at[j], prod, wide, band)

    pass_on(1)

    @pl.loop(0, 2)
    def _(m):
        kind = core * 2 + m

        @pl.when(jnp.logical_not((below | above) & (kind == own_kind)))
        def _():
            rim_in(kind).wait_recv()
            rim_inward(kind).start()

    pass_on(2)
    passed_on(1)
    passed_on(2)

    @pl.loop(0, 2)
    def _(m):
        rim_inward((1 - core) * 2 + m).wait_recv()
        rim_inward(core * 2 + m).wait_send()

    to_sibling(0).wait_send()
    to_sibling(1).wait_send()

    @pl.when(core == 0)
    def _():
        first_edges_out(0, sibling).wait_send()

    @pl.when(me == 0)
    def _():
        first_to_sibling.wait_send()

        @pl.loop(1, CHIPS)
        def _(k):
            first_edges_out(k, same_core(k)).wait_send()

    @pl.when(chip == 0)
    def _():
        @pl.loop(1, CHIPS)
        def _(k):
            first_out(k).wait_send()

    @pl.when(below | above)
    def _():
        rim_over(next_tile).wait_send()

        @pl.loop(1, CHIPS)
        def _(i):
            rim_out(other(i)).wait_send()

    for n in range(2):

        @pl.loop(1, CHIPS)
        def _(i):
            gather(n, other(i)).wait_send()

    for n in range(REFS):

        @pl.loop(1, CHIPS)
        def _(i):
            spread_out(n, other(i)).wait_send()
            inward(n, other(i)).wait_send()

        inward(n, chip).wait_send()


def spread(dates, offsets, slc_re, slc_im):
    vmem = pl.BlockSpec(memory_space=pltpu.VMEM)
    hbm = pl.BlockSpec(memory_space=pltpu.HBM)
    dates_all = offsets.shape[0]
    f32 = jnp.float32
    dma = pltpu.SemaphoreType.DMA
    return pl.pallas_call(
        spread_kernel,
        out_shape=(
            jax.ShapeDtypeStruct((REFS, 2, CHIPS, 8, COLS), f32),
            jax.ShapeDtypeStruct((4, 8, COLS), f32),
            jax.ShapeDtypeStruct((2, 8, COLS), f32),
            jax.ShapeDtypeStruct((2, 8, COLS), f32),
            jax.ShapeDtypeStruct((DATE_DEV, 2, BLOCKS, 72, 128), f32),
            jax.ShapeDtypeStruct((DATE_DEV, BLOCKS, ROWS, 128), f32),
            jax.ShapeDtypeStruct((DATE_DEV, ROWS, COLS), f32),
            jax.ShapeDtypeStruct((DATE_DEV, ROWS, COLS), f32),
        ),
        in_specs=[hbm] * 4,
        out_specs=(vmem,) * 8,
        scratch_shapes=[
            pltpu.SMEM((STEPS,), jnp.int32),
            pltpu.SMEM((dates_all,), jnp.int32),
            pltpu.VMEM((DATE_DEV, ROWS, COLS), f32),
            pltpu.VMEM((DATE_DEV, ROWS, COLS), f32),
            pltpu.VMEM((256, 256), jnp.bfloat16),
            pltpu.VMEM((2, BLOCKS, 72, 128), f32),
            pltpu.VMEM((BLOCKS, 2 * ROWS, 256), jnp.bfloat16),
            pltpu.VMEM((2, BLOCKS, 72, 128), f32),
            pltpu.VMEM((BLOCKS, ROWS, 128), f32),
            dma((4,)),
            pltpu.VMEM((8, COLS), f32),
            pltpu.VMEM((2, 8, COLS), f32),
            pltpu.VMEM((2, 8, COLS), f32),
            pltpu.VMEM((8, COLS), f32),
            pltpu.VMEM((REFS, CHIPS, 8, COLS), f32),
            pltpu.VMEM((2, CHIPS, 8, COLS), f32),
            pltpu.VMEM((2, CHIPS, 8, COLS), f32),
            pltpu.VMEM((CHIPS, 8, COLS), f32),
            pltpu.VMEM((2, CHIPS, 8, COLS), f32),
            pltpu.VMEM((CHIPS, 8, COLS), f32),
            pltpu.VMEM((CHIPS, 8, COLS), f32),
            dma((3,)),
            dma((3,)),
            dma((2,)),
            dma((2,)),
            dma((CHIPS,)),
            dma((1,)),
            dma((2, CHIPS)),
            dma((2, CHIPS)),
            dma((REFS, CHIPS)),
            dma((REFS, CHIPS)),
            dma((REFS, CHIPS)),
            dma((REFS, CHIPS)),
            dma((CHIPS + 1,)),
            dma((5,)),
            dma((4,)),
            dma((4,)),
            dma((CHIPS,)),
            dma((1,)),
        ],
        compiler_params=pltpu.CompilerParams(collective_id=0, has_side_effects=True, vmem_limit_bytes=VMEM_LIMIT),
        name="spread",
    )(dates, offsets, slc_re, slc_im)


def compute_kernel(
    dates_hbm,
    keep_hbm,
    re_hbm,
    im_hbm,
    left,
    right,
    refs,
    ref_edges,
    b_ext,
    pow_b,
    first_re,
    first_im,
    out_re,
    out_im,
    dates_ref,
    keep_ref,
    band,
    own,
    zeros,
    stage,
    a_ext,
    prod,
    wide,
    pow_a,
    own_sems,
    out_sems,
):
    me = lax.axis_index("date")
    tile = lax.axis_index("tile")
    has_top = (tile > 0).astype(jnp.float32)
    has_bottom = (tile < lax.axis_size("tile") - 1).astype(jnp.float32)
    outs = (out_re, out_im)

    def zero_out(s, j, p):
        return pltpu.make_async_copy(zeros, outs[p].at[s, j], out_sems.at[p, s, j])

    def value_out(s, j, p):
        return pltpu.make_async_copy(stage.at[p, s - 1, j], outs[p].at[s, j], out_sems.at[p, s, j])

    def first_out(j, p):
        return pltpu.make_async_copy((first_re, first_im)[p].at[j], outs[p].at[0, j], out_sems.at[p, 0, j])

    slot = DATE_DEV - 2
    own_loads = [pltpu.make_async_copy(h.at[slot], own.at[p], own_sems.at[p]) for p, h in enumerate((re_hbm, im_hbm))]

    def past_last(j):
        return me * DATE_DEV + j == lax.axis_size("date") * DATE_DEV - 1

    def valid(s, j):
        date = me * DATE_DEV + j
        return (keep_ref[s, date] == 1) & (date > dates_ref[s]) & ((s < REFS) | past_last(j))

    scalars = ((dates_hbm, dates_ref), (keep_hbm, keep_ref))
    loads = [pltpu.make_async_copy(a, b, own_sems.at[2 + k]) for k, (a, b) in enumerate(scalars)]
    for c in loads:
        c.start()
    zeros[...] = jnp.zeros_like(zeros)

    @pl.loop(0, DATE_DEV)
    def _(j):
        @pl.when(jnp.logical_not(past_last(j)))
        def _():
            zero_out(REFS, j, 0).start()
            zero_out(REFS, j, 1).start()

    def edge_rows(tile_rows, at):
        return jnp.where(at == 0, tile_rows[0:2], jnp.where(at == 1, tile_rows[2:4], tile_rows[4:6]))

    def lay_reference(at):
        for p in range(2):
            rows = refs[at, :, 4 * p : 4 * p + 4].reshape(ROWS, COLS)
            top = edge_rows(ref_edges[2 + p], at) * has_top
            bottom = edge_rows(ref_edges[p], at) * has_bottom
            lay(a_ext, p, rows, top, bottom)

    band[...] = band_matrix()

    lay_reference(1)
    power(a_ext, pow_a, prod, wide, band)
    for c in loads:
        c.wait()

    @pl.loop(0, STEPS)
    def _(s):
        @pl.loop(0, DATE_DEV)
        def _(j):
            @pl.when(jnp.logical_not(valid(s, j)) & ((s < REFS) | past_last(j)))
            def _():
                zero_out(s, j, 0).start()
                zero_out(s, j, 1).start()

    @pl.loop(0, DATE_DEV)
    def _(j):
        @pl.when(valid(0, j))
        def _():
            first_out(j, 0).start()
            first_out(j, 1).start()

    last = valid(REFS, DATE_DEV - 1)

    @pl.when(last)
    def _():
        for c in own_loads:
            c.start()

    @pl.loop(1, STEPS)
    def _(s):
        some = valid(s, 0) | valid(s, 1) | valid(s, 2) | valid(s, 3)

        @pl.when(some & (s > 1) & (s < REFS))
        def _():
            lay_reference(REFS - 1)

        @pl.when(some & (s == REFS))
        def _():
            for c in own_loads:
                c.wait()
            for p in range(2):
                top = left[slot // 2, 2 * p : 2 * p + 2] * has_top
                bottom = right[slot // 2, 2 * p : 2 * p + 2] * has_bottom
                lay(a_ext, p, own[p], top, bottom)

        @pl.when(some & (s > 1))
        def _():
            power(a_ext, pow_a, prod, wide, band)

        @pl.loop(0, DATE_DEV)
        def _(j):
            @pl.when(valid(s, j))
            def _():
                coherence(a_ext, pow_a, b_ext.at[j], pow_b.at[j], stage.at[0, s - 1, j], stage.at[1, s - 1, j], prod, wide, band)
                value_out(s, j, 0).start()
                value_out(s, j, 1).start()

    @pl.loop(0, STEPS)
    def _(s):
        @pl.loop(0, DATE_DEV)
        def _(j):
            zero_out(s, j, 0).wait()
            zero_out(s, j, 1).wait()


def compute(dates, keep, slc_re, slc_im, *parts):
    vmem = pl.BlockSpec(memory_space=pltpu.VMEM)
    hbm = pl.BlockSpec(memory_space=pltpu.HBM)
    shape = jax.ShapeDtypeStruct((STEPS, DATE_DEV, ROWS, COLS), jnp.float32)
    f32 = jnp.float32
    return pl.pallas_call(
        compute_kernel,
        out_shape=(shape, shape),
        in_specs=[hbm] * 4 + [vmem] * len(parts),
        out_specs=(hbm, hbm),
        scratch_shapes=[
            pltpu.SMEM((STEPS,), jnp.int32),
            pltpu.SMEM(keep.shape, jnp.int32),
            pltpu.VMEM((256, 256), jnp.bfloat16),
            pltpu.VMEM((2, ROWS, COLS), f32),
            pltpu.VMEM((ROWS, COLS), f32),
            pltpu.VMEM((2, REFS, DATE_DEV, ROWS, COLS), f32),
            pltpu.VMEM((2, BLOCKS, 72, 128), f32),
            pltpu.VMEM((2, BLOCKS, 72, 128), f32),
            pltpu.VMEM((BLOCKS, 2 * ROWS, 256), jnp.bfloat16),
            pltpu.VMEM((BLOCKS, ROWS, 128), f32),
            pltpu.SemaphoreType.DMA((4,)),
            pltpu.SemaphoreType.DMA((2, STEPS, DATE_DEV)),
        ],
        compiler_params=pltpu.CompilerParams(vmem_limit_bytes=VMEM_LIMIT),
        name="coherence",
    )(dates, keep, slc_re, slc_im, *parts)


def body(slc_re, slc_im, ref_dates, pair_keep, col_offsets):
    hbm = [pltpu.with_memory_space_constraint(x, pltpu.HBM) for x in (slc_re, slc_im, ref_dates, pair_keep, col_offsets)]
    slc_re, slc_im, ref_dates, pair_keep, col_offsets = hbm
    parts = spread(ref_dates, col_offsets, slc_re, slc_im)
    order = (2, 3, 0, 1, 4, 5, 6, 7)
    return compute(ref_dates, pair_keep, slc_re, slc_im, *[parts[k] for k in order])


def solution(mesh):
    placed = (P("date", "tile", None), P("date", "tile", None), P(), P(), P())
    return jax.shard_map(
        body,
        mesh=mesh,
        in_specs=placed,
        out_specs=(P(None, "date", "tile", None), P(None, "date", "tile", None)),
        check_vma=False,
    )
```

```python
import jax
import jax.numpy as jnp
from jax import lax
from jax.experimental import pallas as pl
from jax.experimental.pallas import tpu as pltpu
from jax.sharding import PartitionSpec as P

MESH = pl.DeviceIdType.MESH
DATE_DEV = 4
ROWS = 64
COLS = 1024
BLOCKS = COLS // 128
REFS = 3
STEPS = 4
VMEM_LIMIT = 24 * 2**20


def band_matrix():
    k = lax.rem(lax.broadcasted_iota(jnp.int32, (256, 256), 0), 128)
    c = lax.broadcasted_iota(jnp.int32, (256, 256), 1)
    within = (c < 128) & (k >= c - 10) & (k <= c + 9)
    after = (c >= 128) & (c < 138) & (k >= c - 10)
    before = (c >= 247) & (k <= c - 247)
    return jnp.where(within | after | before, 1.0, 0.0).astype(jnp.bfloat16)


def lay(ext, plane, rows, top, bottom):
    for g in range(BLOCKS):
        cut = slice(128 * g, 128 * g + 128)
        ext[plane, g, 0:2] = top[:, cut]
        ext[plane, g, 2 : ROWS + 2] = rows[:, cut]
        ext[plane, g, ROWS + 2 : ROWS + 4] = bottom[:, cut]


def widen(prod, wide, count):
    for g in range(BLOCKS):
        for p in range(count):
            total = prod[p, g, 0:ROWS]
            for k in range(1, 5):
                total = total + prod[p, g, k : k + ROWS]
            high = total.astype(jnp.bfloat16)
            low = (total - high.astype(jnp.float32)).astype(jnp.bfloat16)
            wide[g, p * ROWS : (p + 1) * ROWS, 0:128] = high
            wide[g, p * ROWS : (p + 1) * ROWS, 128:256] = low


def columns(wide, band, count):
    rows = count * ROWS
    lhs = wide[:, 0:rows, :].reshape(BLOCKS * rows, 256)
    return jnp.dot(lhs, band[...], preferred_element_type=jnp.float32).reshape(BLOCKS, rows, 256)


def joined(sums, g, p):
    lane = lax.broadcasted_iota(jnp.int32, (ROWS, 128), 1)
    rows = slice(p * ROWS, (p + 1) * ROWS)
    zero = jnp.zeros((ROWS, 128), jnp.float32)
    before = sums[g - 1, rows, 128:256] if g > 0 else zero
    after = sums[g + 1, rows, 128:256] if g < BLOCKS - 1 else zero
    return sums[g, rows, 0:128] + jnp.where(lane < 64, before, after)


def power(ext, out, prod, wide, band):
    for g in range(BLOCKS):
        prod[0, g] = ext[0, g] * ext[0, g] + ext[1, g] * ext[1, g]
    widen(prod, wide, 1)
    sums = columns(wide, band, 1)
    for g in range(BLOCKS):
        out[g] = joined(sums, g, 0)


def coherence(a_ext, pow_a, b_ext, pow_b, out_re, out_im, prod, wide, band):
    for g in range(BLOCKS):
        a_re, a_im = a_ext[0, g], a_ext[1, g]
        b_re, b_im = b_ext[0, g], b_ext[1, g]
        prod[0, g] = a_re * b_re + a_im * b_im
        prod[1, g] = a_im * b_re - a_re * b_im
    widen(prod, wide, 2)
    sums = columns(wide, band, 2)
    for g in range(BLOCKS):
        scale = lax.rsqrt(pow_a[g] * pow_b[g] + 1e-06)
        for p, out in ((0, out_re), (1, out_im)):
            out[:, 128 * g : 128 * g + 128] = joined(sums, g, p) * scale


CHIPS = 8


def spread_kernel(
    dates_hbm,
    offsets_hbm,
    re_hbm,
    im_hbm,
    refs,
    ref_edges,
    left,
    right,
    b_ext,
    pow_b,
    first_re,
    first_im,
    dates_ref,
    offsets_ref,
    re_ref,
    im_ref,
    band,
    prod,
    wide,
    a_ext,
    pow_a,
    load_sems,
    first_edges,
    edges_right,
    edges_left,
    packed,
    outward,
    second_halves,
    third_halves,
    first_half,
    merged,
    second_pieces,
    third_pieces,
    pair_send,
    pair_recv,
    edge_send,
    edge_recv,
    first_send,
    first_recv,
    gather_send,
    gather_recv,
    spread_send,
    spread_recv,
    inward_send,
    inward_recv,
    rim_send,
    rim_recv,
    rim_in_send,
    rim_in_recv,
    top_send,
    top_recv,
):
    me = lax.axis_index("date")
    tile = lax.axis_index("tile")
    chip, core = me // 2, me % 2
    halves = (second_halves, third_halves)
    pieces = (second_pieces, third_pieces)
    tiles = lax.axis_size("tile")
    next_tile = {"tile": lax.rem(tile + 1, tiles)}
    last_tile = {"tile": lax.rem(tile + tiles - 1, tiles)}
    sibling = {"date": chip * 2 + 1 - core}

    def same_core(k):
        return {"date": k * 2 + core}

    def other(i):
        return lax.rem(chip + i, CHIPS)

    def sender(i):
        return lax.rem(chip + CHIPS - i, CHIPS)

    def remote(source, target, send, recv, to):
        return pltpu.make_async_remote_copy(src_ref=source, dst_ref=target, send_sem=send, recv_sem=recv, device_id=to, device_id_type=MESH)

    sources = ((dates_hbm, dates_ref), (offsets_hbm, offsets_ref), (re_hbm, re_ref), (im_hbm, im_ref))
    loads = [pltpu.make_async_copy(a, b, load_sems.at[k]) for k, (a, b) in enumerate(sources)]
    for c in loads:
        c.start()

    barrier = pltpu.get_barrier_semaphore()

    def greet(target):
        pl.semaphore_signal(barrier, inc=1, device_id=target, device_id_type=MESH)

    @pl.loop(1, CHIPS)
    def _(i):
        greet(same_core(other(i)))

    greet(next_tile)
    greet(last_tile)
    greet(sibling)
    band[...] = band_matrix()

    for c in loads:
        c.wait()

    def half(slot, c):
        rows = pl.ds(pl.multiple_of(c * 32, 32), 32)
        return re_ref[slot, rows].reshape(4, 8, COLS), im_ref[slot, rows].reshape(4, 8, COLS)

    for s in range(1, REFS):
        slot = lax.rem(dates_ref[s], DATE_DEV)
        halves[s - 1][core, 0:4], halves[s - 1][core, 4:8] = half(slot, core)
        outward[s - 1, 0:4], outward[s - 1, 4:8] = half(slot, 1 - core)

    @pl.when(me == 0)
    def _():
        first_half[0:4], first_half[4:8] = half(0, 0)
        outward[REFS - 1, 0:4], outward[REFS - 1, 4:8] = half(0, 1)

    for j in range(DATE_DEV):
        at = 4 * (j % 2)
        for p, plane in enumerate((re_ref, im_ref)):
            edges_right[j // 2, at + 2 * p : at + 2 * p + 2] = plane[j, ROWS - 2 : ROWS]
            edges_left[j // 2, at + 2 * p : at + 2 * p + 2] = plane[j, 0:2]

    pl.semaphore_wait(barrier, 10)

    def to_sibling(n):
        return remote(outward.at[n], halves[n].at[core], pair_send.at[n], pair_recv.at[n], sibling)

    first_to_sibling = remote(outward.at[REFS - 1], first_half, pair_send.at[2], pair_recv.at[2], sibling)
    to_sibling(0).start()
    to_right = remote(edges_right, left, edge_send.at[0], edge_recv.at[0], next_tile)
    to_left = remote(edges_left, right, edge_send.at[1], edge_recv.at[1], last_tile)
    to_right.start()
    to_left.start()

    def first_out(k):
        return remote(first_half.at[k], refs.at[0, core, k], first_send.at[k], first_recv.at[0], same_core(k))

    def first_all():
        refs[0, core, 0] = first_half[0]

        @pl.loop(1, CHIPS)
        def _(k):
            first_out(k).start()

    @pl.when(me == 0)
    def _():
        first_to_sibling.start()
        first_all()

    to_sibling(1).start()

    def gather(n, k):
        return remote(merged.at[n, k], pieces[n].at[chip], gather_send.at[n, k], gather_recv.at[n, chip], same_core(k))

    def gathered(n, k):
        return remote(merged.at[n, k], pieces[n].at[k], gather_send.at[n, k], gather_recv.at[n, k], same_core(k))

    @pl.when(me == 1)
    def _():
        first_to_sibling.wait_recv()
        first_all()

    for n in range(2):
        to_sibling(n).wait_recv()
        owner_core = lax.rem(dates_ref[n + 1] // DATE_DEV, 2)
        merged[n] = halves[n][owner_core]

        @pl.loop(1, CHIPS)
        def _(i):
            gather(n, other(i)).start()

        pieces[n][chip] = merged[n, chip]

    def part(n, k):
        return refs.at[n, core, k]

    def spread_out(n, k):
        return remote(part(n, chip), part(n, chip), spread_send.at[n, k], spread_recv.at[n, chip], same_core(k))

    def spread_in(n, k):
        return remote(part(n, k), part(n, k), spread_send.at[n, k], spread_recv.at[n, k], same_core(k))

    def inward(n, k):
        return remote(part(n, k), part(n, k), inward_send.at[n, k], inward_recv.at[n, k], sibling)

    def inward_in(n, k):
        there = refs.at[n, 1 - core, k]
        return remote(there, there, inward_send.at[n, k], inward_recv.at[n, k], sibling)

    def spread_all(n):
        @pl.loop(1, CHIPS)
        def _(i):
            spread_out(n, other(i)).start()

        inward(n, chip).start()

    @pl.when(chip > 0)
    def _():
        first_out(chip).wait_recv()

    spread_all(0)

    to_right.wait()
    to_left.wait()
    has_top = (tile > 0).astype(jnp.float32)
    has_bottom = (tile < tiles - 1).astype(jnp.float32)

    def first_edges_out(k, to):
        return remote(first_edges, first_edges, top_send.at[k], top_recv.at[0], to)

    @pl.when(me == 0)
    def _():
        first_edges[0:4] = left[0, 0:4]
        first_edges[4:8] = right[0, 0:4]

        @pl.loop(1, CHIPS)
        def _(k):
            first_edges_out(k, same_core(k)).start()

        first_edges_out(0, sibling).start()

    def take(n):
        @pl.loop(1, CHIPS)
        def _(i):
            gathered(n, sender(i)).wait_recv()

        refs[n + 1, core, chip] = pieces[n][dates_ref[n + 1] // (2 * DATE_DEV)]

    take(0)
    spread_all(1)
    take(1)

    below = (core == 0) & (lax.rem(chip, 4) == 0)
    above = (core == 1) & (lax.rem(chip, 4) == 3)
    own_kind = jnp.where(core == 0, 0, 2) + chip // 4

    def rim_over(to):
        return remote(packed, ref_edges.at[own_kind], rim_send.at[0], rim_recv.at[4], to)

    @pl.when(below)
    def _():
        for s in range(REFS):
            packed[2 * s : 2 * s + 2] = refs[s, core, chip, 0:2]
        packed[6:8] = jnp.zeros((2, COLS), jnp.float32)
        rim_over(last_tile).start()

    @pl.when(above)
    def _():
        for s in range(REFS):
            packed[2 * s : 2 * s + 2] = refs[s, core, chip, 6:8]
        packed[6:8] = jnp.zeros((2, COLS), jnp.float32)
        rim_over(next_tile).start()

    def rim_out(k):
        return remote(ref_edges.at[own_kind], ref_edges.at[own_kind], rim_send.at[1 + k], rim_recv.at[own_kind], same_core(k))

    def rim_in(kind):
        return remote(ref_edges.at[kind], ref_edges.at[kind], rim_send.at[0], rim_recv.at[kind], sibling)

    def rim_inward(kind):
        return remote(ref_edges.at[kind], ref_edges.at[kind], rim_in_send.at[kind], rim_in_recv.at[kind], sibling)

    @pl.when(below | above)
    def _():
        rim_over(next_tile).wait_recv()

        @pl.loop(1, CHIPS)
        def _(i):
            rim_out(other(i)).start()

        rim_inward(own_kind).start()

    spread_all(2)

    def pass_on(n):
        @pl.loop(1, CHIPS)
        def _(i):
            k = sender(i)
            spread_in(n, k).wait_recv()
            inward(n, k).start()

    def passed_on(n):
        @pl.loop(0, CHIPS)
        def _(k):
            inward_in(n, k).wait_recv()

    @pl.when(me > 0)
    def _():
        first_edges_out(0, sibling).wait_recv()

    @pl.when((me > 0) & (core == 0))
    def _():
        first_edges_out(0, sibling).start()

    pass_on(0)

    @pl.loop(0, DATE_DEV)
    def _(j):
        offset = offsets_ref[me * DATE_DEV + j]

        def shifted(x):
            for step in (1, 2, 4):
                x = jnp.where(lax.rem(offset // step, 2) == 1, pltpu.roll(x, COLS - step, 1), x)
            column = lax.broadcasted_iota(jnp.int32, x.shape, 1)
            return jnp.where(column < COLS - offset, x, 0.0)

        def edges_of(side):
            both = side[j // 2]
            return jnp.where(lax.rem(j, 2) == 0, both[0:4], both[4:8])

        above_rows = shifted(edges_of(left)) * has_top
        below_rows = shifted(edges_of(right)) * has_bottom
        lay(b_ext.at[j], 0, shifted(re_ref[j]), above_rows[0:2], below_rows[0:2])
        lay(b_ext.at[j], 1, shifted(im_ref[j]), above_rows[2:4], below_rows[2:4])
        power(b_ext.at[j], pow_b.at[j], prod, wide, band)

    passed_on(0)
    for p in range(2):
        rows = refs[0, :, 4 * p : 4 * p + 4].reshape(ROWS, COLS)
        top = first_edges[2 * p : 2 * p + 2] * has_top
        bottom = first_edges[2 * p + 4 : 2 * p + 6] * has_bottom
        lay(a_ext, p, rows, top, bottom)
    power(a_ext, pow_a, prod, wide, band)

    @pl.loop(0, DATE_DEV)
    def _(j):
        coherence(a_ext, pow_a, b_ext.at[j], pow_b.at[j], first_re.at[j], first_im.at[j], prod, wide, band)

    pass_on(1)

    @pl.loop(0, 2)
    def _(m):
        kind = core * 2 + m

        @pl.when(jnp.logical_not((below | above) & (kind == own_kind)))
        def _():
            rim_in(kind).wait_recv()
            rim_inward(kind).start()

    pass_on(2)
    passed_on(1)
    passed_on(2)

    @pl.loop(0, 2)
    def _(m):
        rim_inward((1 - core) * 2 + m).wait_recv()
        rim_inward(core * 2 + m).wait_send()

    to_sibling(0).wait_send()
    to_sibling(1).wait_send()

    @pl.when(core == 0)
    def _():
        first_edges_out(0, sibling).wait_send()

    @pl.when(me == 0)
    def _():
        first_to_sibling.wait_send()

        @pl.loop(1, CHIPS)
        def _(k):
            first_edges_out(k, same_core(k)).wait_send()

    @pl.when(chip == 0)
    def _():
        @pl.loop(1, CHIPS)
        def _(k):
            first_out(k).wait_send()

    @pl.when(below | above)
    def _():
        rim_over(next_tile).wait_send()

        @pl.loop(1, CHIPS)
        def _(i):
            rim_out(other(i)).wait_send()

    for n in range(2):

        @pl.loop(1, CHIPS)
        def _(i):
            gather(n, other(i)).wait_send()

    for n in range(REFS):

        @pl.loop(1, CHIPS)
        def _(i):
            spread_out(n, other(i)).wait_send()
            inward(n, other(i)).wait_send()

        inward(n, chip).wait_send()


def spread(dates, offsets, slc_re, slc_im):
    vmem = pl.BlockSpec(memory_space=pltpu.VMEM)
    hbm = pl.BlockSpec(memory_space=pltpu.HBM)
    dates_all = offsets.shape[0]
    f32 = jnp.float32
    dma = pltpu.SemaphoreType.DMA
    return pl.pallas_call(
        spread_kernel,
        out_shape=(
            jax.ShapeDtypeStruct((REFS, 2, CHIPS, 8, COLS), f32),
            jax.ShapeDtypeStruct((4, 8, COLS), f32),
            jax.ShapeDtypeStruct((2, 8, COLS), f32),
            jax.ShapeDtypeStruct((2, 8, COLS), f32),
            jax.ShapeDtypeStruct((DATE_DEV, 2, BLOCKS, 72, 128), f32),
            jax.ShapeDtypeStruct((DATE_DEV, BLOCKS, ROWS, 128), f32),
            jax.ShapeDtypeStruct((DATE_DEV, ROWS, COLS), f32),
            jax.ShapeDtypeStruct((DATE_DEV, ROWS, COLS), f32),
        ),
        in_specs=[hbm] * 4,
        out_specs=(vmem,) * 8,
        scratch_shapes=[
            pltpu.SMEM((STEPS,), jnp.int32),
            pltpu.SMEM((dates_all,), jnp.int32),
            pltpu.VMEM((DATE_DEV, ROWS, COLS), f32),
            pltpu.VMEM((DATE_DEV, ROWS, COLS), f32),
            pltpu.VMEM((256, 256), jnp.bfloat16),
            pltpu.VMEM((2, BLOCKS, 72, 128), f32),
            pltpu.VMEM((BLOCKS, 2 * ROWS, 256), jnp.bfloat16),
            pltpu.VMEM((2, BLOCKS, 72, 128), f32),
            pltpu.VMEM((BLOCKS, ROWS, 128), f32),
            dma((4,)),
            pltpu.VMEM((8, COLS), f32),
            pltpu.VMEM((2, 8, COLS), f32),
            pltpu.VMEM((2, 8, COLS), f32),
            pltpu.VMEM((8, COLS), f32),
            pltpu.VMEM((REFS, CHIPS, 8, COLS), f32),
            pltpu.VMEM((2, CHIPS, 8, COLS), f32),
            pltpu.VMEM((2, CHIPS, 8, COLS), f32),
            pltpu.VMEM((CHIPS, 8, COLS), f32),
            pltpu.VMEM((2, CHIPS, 8, COLS), f32),
            pltpu.VMEM((CHIPS, 8, COLS), f32),
            pltpu.VMEM((CHIPS, 8, COLS), f32),
            dma((3,)),
            dma((3,)),
            dma((2,)),
            dma((2,)),
            dma((CHIPS,)),
            dma((1,)),
            dma((2, CHIPS)),
            dma((2, CHIPS)),
            dma((REFS, CHIPS)),
            dma((REFS, CHIPS)),
            dma((REFS, CHIPS)),
            dma((REFS, CHIPS)),
            dma((CHIPS + 1,)),
            dma((5,)),
            dma((4,)),
            dma((4,)),
            dma((CHIPS,)),
            dma((1,)),
        ],
        compiler_params=pltpu.CompilerParams(collective_id=0, has_side_effects=True, vmem_limit_bytes=VMEM_LIMIT),
        name="spread",
    )(dates, offsets, slc_re, slc_im)


def compute_kernel(
    dates_hbm,
    keep_hbm,
    re_hbm,
    im_hbm,
    left,
    right,
    refs,
    ref_edges,
    b_ext,
    pow_b,
    first_re,
    first_im,
    out_re,
    out_im,
    dates_ref,
    keep_ref,
    band,
    own,
    zeros,
    stage,
    a_ext,
    prod,
    wide,
    pow_a,
    own_sems,
    out_sems,
):
    me = lax.axis_index("date")
    tile = lax.axis_index("tile")
    has_top = (tile > 0).astype(jnp.float32)
    has_bottom = (tile < lax.axis_size("tile") - 1).astype(jnp.float32)
    outs = (out_re, out_im)

    def zero_out(s, j, p):
        return pltpu.make_async_copy(zeros, outs[p].at[s, j], out_sems.at[p, s, j])

    def value_out(s, j, p):
        return pltpu.make_async_copy(stage.at[p, s - 1, j], outs[p].at[s, j], out_sems.at[p, s, j])

    def first_out(j, p):
        return pltpu.make_async_copy((first_re, first_im)[p].at[j], outs[p].at[0, j], out_sems.at[p, 0, j])

    slot = DATE_DEV - 2
    own_loads = [pltpu.make_async_copy(h.at[slot], own.at[p], own_sems.at[p]) for p, h in enumerate((re_hbm, im_hbm))]

    def past_last(j):
        return me * DATE_DEV + j == lax.axis_size("date") * DATE_DEV - 1

    def valid(s, j):
        date = me * DATE_DEV + j
        return (keep_ref[s, date] == 1) & (date > dates_ref[s]) & ((s < REFS) | past_last(j))

    scalars = ((dates_hbm, dates_ref), (keep_hbm, keep_ref))
    loads = [pltpu.make_async_copy(a, b, own_sems.at[2 + k]) for k, (a, b) in enumerate(scalars)]
    for c in loads:
        c.start()
    zeros[...] = jnp.zeros_like(zeros)

    @pl.loop(0, DATE_DEV)
    def _(j):
        @pl.when(jnp.logical_not(past_last(j)))
        def _():
            zero_out(REFS, j, 0).start()
            zero_out(REFS, j, 1).start()

    def edge_rows(tile_rows, at):
        return jnp.where(at == 0, tile_rows[0:2], jnp.where(at == 1, tile_rows[2:4], tile_rows[4:6]))

    def lay_reference(at):
        for p in range(2):
            rows = refs[at, :, 4 * p : 4 * p + 4].reshape(ROWS, COLS)
            top = edge_rows(ref_edges[2 + p], at) * has_top
            bottom = edge_rows(ref_edges[p], at) * has_bottom
            lay(a_ext, p, rows, top, bottom)

    band[...] = band_matrix()

    lay_reference(1)
    power(a_ext, pow_a, prod, wide, band)
    for c in loads:
        c.wait()

    @pl.loop(0, STEPS)
    def _(s):
        @pl.loop(0, DATE_DEV)
        def _(j):
            @pl.when(jnp.logical_not(valid(s, j)) & ((s < REFS) | past_last(j)))
            def _():
                zero_out(s, j, 0).start()
                zero_out(s, j, 1).start()

    @pl.loop(0, DATE_DEV)
    def _(j):
        @pl.when(valid(0, j))
        def _():
            first_out(j, 0).start()
            first_out(j, 1).start()

    last = valid(REFS, DATE_DEV - 1)

    @pl.when(last)
    def _():
        for c in own_loads:
            c.start()

    @pl.loop(1, STEPS)
    def _(s):
        some = valid(s, 0) | valid(s, 1) | valid(s, 2) | valid(s, 3)

        @pl.when(some & (s > 1) & (s < REFS))
        def _():
            lay_reference(REFS - 1)

        @pl.when(some & (s == REFS))
        def _():
            for c in own_loads:
                c.wait()
            for p in range(2):
                top = left[slot // 2, 2 * p : 2 * p + 2] * has_top
                bottom = right[slot // 2, 2 * p : 2 * p + 2] * has_bottom
                lay(a_ext, p, own[p], top, bottom)

        @pl.when(some & (s > 1))
        def _():
            power(a_ext, pow_a, prod, wide, band)

        @pl.loop(0, DATE_DEV)
        def _(j):
            @pl.when(valid(s, j))
            def _():
                coherence(a_ext, pow_a, b_ext.at[j], pow_b.at[j], stage.at[0, s - 1, j], stage.at[1, s - 1, j], prod, wide, band)
                value_out(s, j, 0).start()
                value_out(s, j, 1).start()

    @pl.loop(0, STEPS)
    def _(s):
        @pl.loop(0, DATE_DEV)
        def _(j):
            zero_out(s, j, 0).wait()
            zero_out(s, j, 1).wait()


def compute(dates, keep, slc_re, slc_im, *parts):
    vmem = pl.BlockSpec(memory_space=pltpu.VMEM)
    hbm = pl.BlockSpec(memory_space=pltpu.HBM)
    shape = jax.ShapeDtypeStruct((STEPS, DATE_DEV, ROWS, COLS), jnp.float32)
    f32 = jnp.float32
    return pl.pallas_call(
        compute_kernel,
        out_shape=(shape, shape),
        in_specs=[hbm] * 4 + [vmem] * len(parts),
        out_specs=(hbm, hbm),
        scratch_shapes=[
            pltpu.SMEM((STEPS,), jnp.int32),
            pltpu.SMEM(keep.shape, jnp.int32),
            pltpu.VMEM((256, 256), jnp.bfloat16),
            pltpu.VMEM((2, ROWS, COLS), f32),
            pltpu.VMEM((ROWS, COLS), f32),
            pltpu.VMEM((2, REFS, DATE_DEV, ROWS, COLS), f32),
            pltpu.VMEM((2, BLOCKS, 72, 128), f32),
            pltpu.VMEM((2, BLOCKS, 72, 128), f32),
            pltpu.VMEM((BLOCKS, 2 * ROWS, 256), jnp.bfloat16),
            pltpu.VMEM((BLOCKS, ROWS, 128), f32),
            pltpu.SemaphoreType.DMA((4,)),
            pltpu.SemaphoreType.DMA((2, STEPS, DATE_DEV)),
        ],
        compiler_params=pltpu.CompilerParams(vmem_limit_bytes=VMEM_LIMIT),
        name="coherence",
    )(dates, keep, slc_re, slc_im, *parts)


def body(slc_re, slc_im, ref_dates, pair_keep, col_offsets):
    hbm = [pltpu.with_memory_space_constraint(x, pltpu.HBM) for x in (slc_re, slc_im, ref_dates, pair_keep, col_offsets)]
    slc_re, slc_im, ref_dates, pair_keep, col_offsets = hbm
    parts = spread(ref_dates, col_offsets, slc_re, slc_im)
    order = (2, 3, 0, 1, 4, 5, 6, 7)
    return compute(ref_dates, pair_keep, slc_re, slc_im, *[parts[k] for k in order])


def solution(mesh):
    placed = (P("date", "tile", None), P("date", "tile", None), P(), P(), P())
    return jax.shard_map(
        body,
        mesh=mesh,
        in_specs=placed,
        out_specs=(P(None, "date", "tile", None), P(None, "date", "tile", None)),
        check_vma=False,
    )
```
